512 devices in a mesh: span: 32 (over y, z_lo), head: 16 (over x, z_hi, core).
Axes of the slice: x: 4, y: 4, z: 16 (z_hi: 2, z_lo: 8; z = z_hi * 8 + z_lo), core: 2. Of those that a mesh axis runs over, the one named last changes fastest.
Arguments:
- query: bfloat16 [12288, 4096], P(('span', 'head'))
- keys: bfloat16 [12288, 4096], P(('span', 'head'))
- values: bfloat16 [12288, 4096], P(('span', 'head')), may hold values from -6 to 6
- out_weight: bfloat16 [4096, 5120], P('head'), may hold values from -0.5 to 0.5
- time_gates: float32 [30, 5120], replicated, may hold values from 0.5 to 2
- noise_step: int32 [32], replicated, may hold values from 0 to 29
- span_length: int32 [32], replicated, may hold values from 96 to 384, as said below
- window_start: int32 [32], replicated, may hold values from 0 to 15, as said below
- latent: float32 [12288, 5120], P(('span', 'head')), may hold values from -6 to 6
Outputs:
- velocity: bfloat16 [12288, 5120], P(('span', 'head'))
- advanced: float32 [12288, 5120], P(('span', 'head'))
The draws below stay inside these ranges and needn't reach their ends.
Inputs may be any that keep to these rules, and one draw needn't show every extreme that they name: `span_length`: every span has at least 96 live tokens, and some span is full. window_start[c] <= c // 2 for every span c, so a span always attends to itself.
All inputs are finite; a program needn't handle non-finite values.
Results may differ from the reference program's by a relative error of at most 0.02.
Values may be sent and summed in bfloat16 or wider, within the bound.
A program may use at most 128 MiB of HBM per device.

```python
import math
import jax
import jax.numpy as jnp
from jax import lax

D = 5120
HEADS = 32
HS = 128
STEPS = 30
SPAN_TOK = 384
SPANS = 32
TOKENS = 12288
N_HEAD = 16


def draw_query(key, part):
    key = jax.random.fold_in(key, 3)
    drawn = jax.random.normal(key, (TOKENS, HEADS * HS), jnp.float32)
    return drawn.astype(jnp.bfloat16)


def draw_keys(key, part):
    key = jax.random.fold_in(key, 5)
    drawn = 1.5 * jax.random.normal(key, (TOKENS, HEADS * HS), jnp.float32)
    return drawn.astype(jnp.bfloat16)


def draw_span_length(key, part):
    key = jax.random.fold_in(key, 7)
    lengths = jax.random.randint(key, (SPANS,), SPAN_TOK // 4, SPAN_TOK + 1, dtype=jnp.int32)
    picked = jax.random.randint(jax.random.fold_in(key, 1), (), 0, SPANS, dtype=jnp.int32)
    return jnp.where(jnp.arange(SPANS, dtype=jnp.int32) == picked, SPAN_TOK, lengths).astype(jnp.int32)


def draw_window_start(key, part):
    key = jax.random.fold_in(key, 9)
    span_ids = jnp.arange(SPANS, dtype=jnp.int32)
    starts = jax.random.randint(key, (SPANS,), 0, span_ids // 2 + 1, dtype=jnp.int32)
    return jnp.where(span_ids == SPANS - 1, (SPANS - 1) // 2, starts).astype(jnp.int32)


def plant(drawn, own_key, least, high):
    shape = drawn.shape
    place = [jax.random.randint(jax.random.fold_in(own_key, axis), (), 0, shape[axis]) for axis in range(len(shape))]
    drawn = drawn.at[tuple(place)].set(least)
    longest = shape.index(max(shape))
    place[longest] = (place[longest] + 1) % shape[longest]
    return drawn.at[tuple(place)].set(high)


def levels(own_key, dims, split, least, high):
    factor_of, own = 1.0, jax.random.fold_in(own_key, 6)
    for dim, shards_of in split:
        steps = jnp.exp(jax.random.uniform(jax.random.fold_in(own, dim), (shards_of,), jnp.float32, least / len(split), high / len(split)))
        factor_of = factor_of * jnp.repeat(steps, dims[dim] // shards_of).reshape([-1 if axis == dim else 1 for axis in range(len(dims))])
    return factor_of


def centred(key, dims, width, bound, pieces=(), kind=jnp.bfloat16):
    factor_of = levels(key, dims, pieces, -0.22, 0.18) if pieces else 1.0
    array = jax.random.normal(key, dims, jnp.float32) * width * factor_of
    return jnp.minimum(jnp.maximum(array, -bound), bound).astype(kind)


def setup_inputs(seed: int = 0) -> dict:
    seeds = jax.random.split(jax.random.key(seed), 10)
    query = draw_query(jax.random.fold_in(seeds[9], 71), 0)
    keys = draw_keys(jax.random.fold_in(seeds[9], 71), 0)
    values = centred(seeds[2], (TOKENS, HEADS * HS), 1.0, 6.0, ((0, 512),))
    out_weight = centred(seeds[3], (HEADS * HS, D), HS ** -0.5, 0.5, ((0, 16),))
    time_gates = jnp.clip(jnp.exp(jax.random.uniform(seeds[4], (STEPS, D), jnp.float32, math.log(0.5), math.log(2.0))), 0.5, 2.0)
    noise_step = plant(jax.random.randint(seeds[5], (SPANS,), 0, STEPS), jax.random.fold_in(seeds[5], 1), 0, STEPS - 1).astype(jnp.int32)
    span_length = draw_span_length(jax.random.fold_in(seeds[9], 71), 0)
    window_start = draw_window_start(jax.random.fold_in(seeds[9], 71), 0)
    latent = centred(seeds[8], (TOKENS, D), 1.0, 6.0, ((0, 512),), jnp.float32)
    return dict(query=query, keys=keys, values=values, out_weight=out_weight, time_gates=time_gates, noise_step=noise_step, span_length=span_length, window_start=window_start, latent=latent)


def sigma_of(step):
    fraction = 1.0 - step.astype(jnp.float32) / STEPS
    return 8.0 * fraction / (1.0 + 7.0 * fraction)

def reference(query, keys, values, out_weight, time_gates, noise_step, span_length, window_start, latent):
    key_heads = keys.astype(jnp.float32).reshape(TOKENS, HEADS, HS)
    value_heads = values.astype(jnp.float32).reshape(TOKENS, HEADS, HS)
    rows = jnp.arange(TOKENS, dtype=jnp.int32)
    owner = rows // SPAN_TOK
    position = rows % SPAN_TOK
    key_length = span_length[owner]

    def one_span(span_id):
        start = (span_id * SPAN_TOK).astype(jnp.int32)
        query_heads = lax.dynamic_slice_in_dim(query, start, SPAN_TOK, 0).astype(jnp.float32).reshape(SPAN_TOK, HEADS, HS)
        score = jnp.einsum('qhd,khd->hqk', query_heads, key_heads) / jnp.sqrt(jnp.float32(HS))
        seen = (owner >= window_start[span_id]) & (owner <= span_id) & (position < key_length)
        top_score = lax.optimization_barrier(jnp.max(jnp.where(seen[None, None, :], score, jnp.float32(-1e+30)), axis=-1))
        weight = jnp.where(seen[None, None, :], jnp.exp(score - top_score[..., None]), jnp.float32(0.0))
        total = lax.optimization_barrier(jnp.sum(weight, axis=-1))
        rounded = lax.optimization_barrier(weight.astype(jnp.bfloat16)).astype(jnp.float32)
        summed = jnp.einsum('hqk,khd->qhd', rounded, value_heads)
        attended = summed / jnp.transpose(total)[..., None]
        return attended.reshape(SPAN_TOK, HEADS * HS).astype(jnp.bfloat16)
    attended = lax.map(one_span, jnp.arange(SPANS, dtype=jnp.int32)).reshape(TOKENS, HEADS * HS)
    group = HEADS * HS // N_HEAD

    def add_group(total, group_id):
        offset = (group_id * group).astype(jnp.int32)
        columns = lax.dynamic_slice_in_dim(attended, offset, group, 1)
        weights = lax.dynamic_slice_in_dim(out_weight, offset, group, 0)
        part = jnp.dot(columns, weights, preferred_element_type=jnp.float32)
        part = lax.optimization_barrier(part.astype(jnp.bfloat16)).astype(jnp.float32)
        return (total + part, None)
    projected, unused = lax.scan(add_group, jnp.zeros((TOKENS, D), jnp.float32), jnp.arange(N_HEAD, dtype=jnp.int32))
    token_step = noise_step[owner]
    gates = time_gates[token_step]
    live = (position < key_length).astype(jnp.float32)
    velocity = (gates * projected * live[:, None]).astype(jnp.bfloat16)
    step_size = sigma_of(token_step + 1) - sigma_of(token_step)
    advanced = latent + step_size[:, None] * velocity.astype(jnp.float32)
    return (velocity, advanced)
```

```python
import functools
import math

import jax
import jax.numpy as jnp
from jax import lax
from jax.experimental import pallas as pl
from jax.experimental.pallas import tpu as pltpu
from jax.sharding import PartitionSpec as P

MESH = pl.DeviceIdType.MESH
F32 = jnp.float32
BF16 = jnp.bfloat16

D = 5120
HS = 128
STEPS = 30
ROWS = 24
HALF = 192
NH = 4
NQ = 4 * HALF
NZ = 16
CHUNK = 640
PIECE = 64
NP = 4
TILE = 256
NEG = -1e30
BIG = 3e38
SCALE = math.log2(math.e) / math.sqrt(HS)


def place(x, y, z, core):
    return (y * 8 + z % 8, 4 * x + 2 * (z // 8) + core)


def main_kernel(
    q_ref, k_ref, v_ref, w_ref, slen_ref, wstart_ref, out_ref,
    send_a, recv_a, stage, kv, qbuf, qt, acc, stat, pos_ref, row_ref, wf,
    obuf, robuf, sbuf, rsbuf, att, fs, send_c, recv_c, send_x, recv_x,
    a_s, a_r, q_s, q_r, ring_s, ring_r, wz_s, wz_r, wy_s, wy_r, o_s, o_r, st_s, st_r, c_s, c_r, x_s, x_r,
):
    span = lax.axis_index("span")
    head = lax.axis_index("head")
    y, zlo = span // 8, span % 8
    x, zhi, core = head // 4, (head // 2) % 2, head % 2
    z = zhi * 8 + zlo
    me = core * 4 + x

    def peer(p):
        return place(p % 4, y, z, p // 4)

    def copy(src, dst, ssem, rsem, dev):
        return pltpu.make_async_remote_copy(
            src_ref=src, dst_ref=dst, send_sem=ssem, recv_sem=rsem, device_id=dev, device_id_type=MESH
        )

    side = (place(x, y, (z + 1) % NZ, core), place(x, y, (z + NZ - 1) % NZ, core))

    def ydev(d):
        return place(x, (y + d) % 4, z, core)

    barrier = pltpu.get_barrier_semaphore()
    partners = [peer((me + d) % 8) for d in range(1, 8)] + [ydev(d) for d in range(1, 4)] + list(side)
    for dev in partners:
        pl.semaphore_signal(barrier, inc=1, device_id=dev, device_id_type=MESH)

    def pack(p, carry):
        for tensor, ref in enumerate((q_ref, k_ref, v_ref)):
            for l in range(NH):
                col = 128 * (8 * (p % 4) + 4 * (l // 2) + 2 * (p // 4) + l % 2)
                stage[0, pl.ds((tensor * NH + l) * ROWS, ROWS), :] = ref[
                    :, pl.ds(pl.multiple_of(col, 128), 128)
                ].astype(F32)
        send_a[p] = stage[0, pl.ds(0, 12 * ROWS), :].astype(BF16)
        return carry

    lax.fori_loop(0, 8, pack, 0)
    pl.semaphore_wait(barrier, len(partners))

    def a_copy(d):
        to = (me + d) % 8
        return copy(send_a.at[to], recv_a.at[me], a_s.at[d - 1], a_r.at[d - 1], peer(to))

    def a_start(d, carry):
        a_copy(d).start()
        return carry

    lax.fori_loop(1, 8, a_start, 0)

    def wz_forward(direction, i):
        c = 2 * y + direction
        rows = pl.ds(pl.multiple_of(i * PIECE, PIECE), PIECE)
        return copy(
            wf.at[c, rows], wf.at[c, rows], wz_s.at[direction, i], wz_r.at[direction, i], side[direction]
        )

    def wz_origin(direction, i):
        c = 2 * y + direction
        rows = pl.ds(pl.multiple_of(i * PIECE, PIECE), PIECE)
        cols = pl.ds(pl.multiple_of(c * CHUNK, 128), CHUNK)
        return copy(
            w_ref.at[rows, cols], wf.at[c, rows], wz_s.at[direction, i], wz_r.at[direction, i], side[direction]
        )

    def wy_copy(direction, i, d):
        c = 2 * y + direction
        rows = pl.ds(pl.multiple_of(i * PIECE, PIECE), PIECE)
        return copy(
            wf.at[c, rows], wf.at[c, rows], wy_s.at[direction, i, d - 1], wy_r.at[direction, i, d - 1], ydev(d)
        )

    for direction in range(2):

        @pl.when(zlo == (7 if direction == 0 else 0))
        def _(direction=direction):
            def go(i, carry):
                wz_origin(direction, i).start()
                return carry

            lax.fori_loop(0, NP, go, 0)

    def weight_point(u):
        for direction in range(2):
            hop = zlo if direction == 0 else 7 - zlo
            i = u - hop

            @pl.when((i >= 0) & (i < NP))
            def _(direction=direction, hop=hop, i=i):
                wz_forward(direction, i).wait_recv()

                @pl.when(hop < 7)
                def _():
                    wz_forward(direction, i).start()

                for d in range(1, 4):
                    wy_copy(direction, i, d).start()

    r = lax.broadcasted_iota(jnp.int32, (HALF, 128), 0)
    rc = jnp.where(r >= 96, 1, 0)
    rem = r - 96 * rc
    rx = jnp.where(rem >= 24, 1, 0) + jnp.where(rem >= 48, 1, 0) + jnp.where(rem >= 72, 1, 0)
    pos_ref[...] = 96 * rx + 24 * rc + rem - 24 * rx
    lane = lax.broadcasted_iota(jnp.int32, (8, NQ), 1)
    ly = jnp.where(lane >= HALF, 1, 0) + jnp.where(lane >= 2 * HALF, 1, 0) + jnp.where(lane >= 3 * HALF, 1, 0)
    row_ref[0] = 8 * ly + zlo
    first = jnp.full((8, NQ), wstart_ref[zlo], jnp.int32)
    for yy in range(1, 4):
        first = jnp.where(ly == yy, wstart_ref[8 * yy + zlo], first)
    row_ref[1] = first
    acc[...] = jnp.zeros(acc.shape, F32)
    stat[pl.ds(0, 4), :] = jnp.full((4, 1024), NEG, F32)
    stat[pl.ds(4, 4), :] = jnp.zeros((4, 1024), F32)

    recv_a[me] = send_a[me]

    def unpack(d, carry):
        src = (me + 8 - d) % 8

        @pl.when(d > 0)
        def _():
            a_copy_in(d).wait_recv()

        rows = recv_a[src].astype(F32)
        at = pl.ds(pl.multiple_of(src * ROWS, 8), ROWS)
        for tensor in range(3):
            for l in range(NH):
                n = (tensor * NH + l) * ROWS
                stage[tensor * NH + l, at, :] = rows[n : n + ROWS]
        return carry

    def a_copy_in(d):
        src = (me + 8 - d) % 8
        return copy(send_a.at[src], recv_a.at[src], a_s.at[d - 1], a_r.at[d - 1], peer(src))

    lax.fori_loop(0, 8, unpack, 0)

    def ring_copy(direction, ab, n):
        block = (z + NZ - (n - 1)) % NZ if direction == 0 else (z + n - 1) % NZ
        ref = kv.at[(direction + ab) % 2, block]
        return copy(ref, ref, ring_s.at[direction, ab, n - 1], ring_r.at[direction, ab, n - 1], side[direction])

    def ring_in(direction, ab, n):
        block = (z + NZ - n) % NZ if direction == 0 else (z + n) % NZ
        ref = kv.at[(direction + ab) % 2, block]
        return copy(ref, ref, ring_s.at[direction, ab, n - 1], ring_r.at[direction, ab, n - 1], side[direction])

    for tensor in range(2):
        for l in range(NH):
            kv[tensor, z, pl.ds(l * HALF, HALF), :] = stage[(tensor + 1) * NH + l, pl.ds(0, HALF), :].astype(BF16)
        ring_copy(0, tensor, 1).start()
        ring_copy(1, 1 - tensor, 1).start()
    for l in range(NH):
        qbuf[y, pl.ds(l * HALF, HALF), :] = stage[l, pl.ds(0, HALF), :].astype(BF16)

    def q_copy(d):
        return copy(qbuf.at[y], qbuf.at[y], q_s.at[d - 1], q_r.at[d - 1], ydev(4 - d))

    def q_in(d):
        src = (y + d) % 4
        return copy(qbuf.at[src], qbuf.at[src], q_s.at[d - 1], q_r.at[d - 1], ydev(d))

    for d in range(1, 4):

        @pl.when(y - d >= 0)
        def _(d=d):
            q_copy(d).start()
            qbuf[y - d] = jnp.zeros((NQ, 128), BF16)

    def point(ab, n, last, u):
        for direction in range(2):
            ring_in(direction, ab, n).wait_recv()

            @pl.when(n < last)
            def _(direction=direction):
                ring_copy(direction, ab, n + 1).start()

        weight_point(u)

    for d in range(1, 4):

        @pl.when(y + d <= 3)
        def _(d=d):
            q_in(d).wait_recv()

    def turn(l, carry):
        rows = pl.ds(pl.multiple_of(l * HALF, 64), HALF)
        q_all = jnp.concatenate([qbuf[yy, rows, :].astype(F32) for yy in range(4)], axis=0)
        qt[l] = q_all.T.astype(BF16)
        return carry

    lax.fori_loop(0, NH, turn, 0)
    point(0, 1, 8, 0)
    point(1, 1, 7, 1)

    def attend(za, zb, low, high):
        sides = []
        for zz in (za, zb):
            j = 8 * y + zz % 8
            cap = jnp.where(pos_ref[...] + 48 * (zz // 8) < slen_ref[j], BIG, NEG).astype(F32)
            cap = jnp.concatenate([cap, cap], axis=1)
            seen = (row_ref[1] <= j) & (j <= row_ref[0])
            sides.append((zz, cap, seen))

        def one_head(l, carry):
            rows = pl.ds(pl.multiple_of(l * HALF, 64), HALF)
            k2 = jnp.concatenate([kv[0, za, rows, :], kv[0, zb, rows, :]], axis=0)
            v2 = jnp.concatenate([kv[1, za, rows, :], kv[1, zb, rows, :]], axis=0).T
            for tile in range(NQ // TILE):
                cols = pl.ds(tile * TILE, TILE)
                s = jnp.dot(k2, qt[l, :, cols], preferred_element_type=F32) * SCALE
                old = stat[pl.ds(l, 1), cols]
                top = old
                parts = []
                for n, (zz, cap, seen) in enumerate(sides):
                    part = jnp.minimum(s[n * HALF : (n + 1) * HALF], cap)
                    vis = seen[0:1, tile * TILE : (tile + 1) * TILE]
                    top = jnp.maximum(top, jnp.where(vis, jnp.max(part, axis=0, keepdims=True), NEG))
                    parts.append((part, vis))
                factor = jnp.exp2(old - top)
                weight = jnp.concatenate(
                    [jnp.exp2(part - jnp.where(vis, top, BIG)) for part, vis in parts], axis=0
                )
                stat[pl.ds(l, 1), cols] = top
                stat[pl.ds(4 + l, 1), cols] = stat[pl.ds(4 + l, 1), cols] * factor + jnp.sum(
                    weight, axis=0, keepdims=True
                )
                acc[l, :, cols] = acc[l, :, cols] * factor + jnp.dot(
                    v2, weight.astype(BF16), preferred_element_type=F32
                )
            return carry

        lax.fori_loop(low, high, one_head, 0)

    def step(t, carry):
        za, zb = (z + NZ - t) % NZ, (z + t) % NZ
        point(0, t + 1, 8, 2 * t)
        attend(za, zb, 0, 2)

        @pl.when(t < 7)
        def _():
            point(1, t + 1, 7, 2 * t + 1)

        attend(za, zb, 2, 4)
        return carry

    lax.fori_loop(1, 8, step, 0)
    attend(z, (z + 8) % NZ, 0, 4)

    def finish(l, carry):
        inv = 1.0 / jnp.maximum(stat[pl.ds(4 + l, 1), pl.ds(0, NQ)], 1e-30)
        o = (acc[l] * inv).T.astype(BF16)
        rows = pl.ds(pl.multiple_of(l * HALF, 64), HALF)
        for yy in range(4):
            obuf[yy, rows, :] = o[yy * HALF : (yy + 1) * HALF]
        return carry

    lax.fori_loop(0, NH, finish, 0)
    stats = stat[...]
    for yy in range(4):
        sbuf[yy] = stats[:, yy * HALF : yy * HALF + 256]

    def o_copy(d):
        to = (y + d) % 4
        return (
            copy(sbuf.at[to], rsbuf.at[y], st_s.at[d - 1], st_r.at[d - 1], ydev(d)),
            copy(obuf.at[to], robuf.at[y], o_s.at[d - 1], o_r.at[d - 1], ydev(d)),
        )

    def o_in(d):
        src = (y + 4 - d) % 4
        return (
            copy(sbuf.at[src], rsbuf.at[src], st_s.at[d - 1], st_r.at[d - 1], ydev(4 - d)),
            copy(obuf.at[src], robuf.at[src], o_s.at[d - 1], o_r.at[d - 1], ydev(4 - d)),
        )

    empty = jnp.where(lax.broadcasted_iota(jnp.int32, (8, 256), 0) < 4, NEG, 0.0).astype(F32)
    for d in range(1, 4):

        @pl.when(y + d <= 3)
        def _(d=d):
            for one in o_copy(d):
                one.start()
            rsbuf[y + d] = empty
            robuf[y + d] = jnp.zeros((NQ, 128), BF16)

    rsbuf[y] = sbuf[y]
    robuf[y] = obuf[y]
    for d in range(1, 4):

        @pl.when(y - d >= 0)
        def _(d=d):
            for one in o_in(d):
                one.wait_recv()

    tops = [rsbuf[yy, pl.ds(0, 4), :] for yy in range(4)]
    best = jnp.maximum(jnp.maximum(tops[0], tops[1]), jnp.maximum(tops[2], tops[3]))
    shares = [rsbuf[yy, pl.ds(4, 4), :] * jnp.exp2(tops[yy] - best) for yy in range(4)]
    whole = shares[0] + shares[1] + shares[2] + shares[3]
    inv = 1.0 / whole
    share = jnp.concatenate([one * inv for one in shares] + [jnp.zeros((112, 256), F32)], axis=0).T
    for l in range(NH):
        o = jnp.zeros((HALF, HS), F32)
        for yy in range(4):
            n = 4 * yy + l
            o = o + share[0:HALF, n : n + 1] * robuf[yy, pl.ds(l * HALF, HALF), :].astype(F32)
        att[l // 2, :, pl.ds((l % 2) * HS, HS)] = o.astype(BF16)

    def wy_wait(n, carry):
        direction, i = n // NP, n % NP
        rows = pl.ds(pl.multiple_of(i * PIECE, PIECE), PIECE)
        for d in range(1, 4):
            c = 2 * ((y + 4 - d) % 4) + direction
            copy(
                wf.at[c, rows], wf.at[c, rows], wy_s.at[direction, i, d - 1], wy_r.at[direction, i, d - 1], ydev(d)
            ).wait_recv()
        return carry

    lax.fori_loop(0, 2 * NP, wy_wait, 0)
    twin = place(x, y, z, 1 - core)

    def c_copy(n):
        return copy(send_c.at[n], recv_c.at[n], c_s.at[n], c_r.at[n], twin)

    def project(n, carry):
        cols = pl.ds(pl.multiple_of(n * CHUNK, 128), CHUNK)
        fs[n] = jnp.dot(att[zhi], w_ref[:, cols], preferred_element_type=F32) + jnp.dot(
            att[1 - zhi], wf[n], preferred_element_type=F32
        )
        send_c[n] = fs[n, pl.ds(pl.multiple_of(96 * (1 - core), 8), 96), :].astype(BF16)
        c_copy(n).start()
        return carry

    lax.fori_loop(0, 8, project, 0)

    def x_copy(g, d):
        to = (x + d) % 4
        return copy(
            send_x.at[g, to], recv_x.at[g, x], x_s.at[g, d - 1], x_r.at[g, d - 1], place(to, y, z, core)
        )

    def x_in(g, d):
        src = (x + 4 - d) % 4
        return copy(
            send_x.at[g, src], recv_x.at[g, src], x_s.at[g, d - 1], x_r.at[g, d - 1], place(src, y, z, core)
        )

    def pair_sum(g, carry):
        own = pl.ds(pl.multiple_of(96 * core, 8), 96)
        parts = []
        for n in range(2):
            c_copy(2 * g + n).wait_recv()
            parts.append(fs[2 * g + n, own, :] + recv_c[2 * g + n].astype(F32))
        for xx in range(4):
            send_x[g, xx] = jnp.concatenate([part[xx * ROWS : (xx + 1) * ROWS] for part in parts], axis=0).astype(BF16)
        for d in (2, 1, 3):
            x_copy(g, d).start()
        return carry

    lax.fori_loop(0, 4, pair_sum, 0)

    def collect(g, carry):
        total = send_x[g, x].astype(F32)
        for d in range(1, 4):
            x_in(g, d).wait_recv()
            total = total + recv_x[g, (x + 4 - d) % 4].astype(F32)
        for n in range(2):
            out_ref[:, pl.ds(pl.multiple_of((2 * g + n) * CHUNK, 128), CHUNK)] = total[n * ROWS : (n + 1) * ROWS]
        return carry

    lax.fori_loop(0, 4, collect, 0)

    def a_end(d, carry):
        a_copy(d).wait_send()
        return carry

    lax.fori_loop(1, 8, a_end, 0)

    def ring_end(n, carry):
        for direction in range(2):
            ring_copy(direction, 0, n).wait_send()

            @pl.when(n < 8)
            def _(direction=direction):
                ring_copy(direction, 1, n).wait_send()

        return carry

    lax.fori_loop(1, 9, ring_end, 0)

    def w_end(i, carry):
        for direction in range(2):
            wz_forward(direction, i).wait_send()
            for d in range(1, 4):
                wy_copy(direction, i, d).wait_send()
        return carry

    lax.fori_loop(0, NP, w_end, 0)
    for d in range(1, 4):

        @pl.when(y - d >= 0)
        def _(d=d):
            q_copy(d).wait_send()

        @pl.when(y + d <= 3)
        def _(d=d):
            for one in o_copy(d):
                one.wait_send()

    def c_end(n, carry):
        c_copy(n).wait_send()
        return carry

    lax.fori_loop(0, 8, c_end, 0)

    def x_end(g, carry):
        for d in range(1, 4):
            x_copy(g, d).wait_send()
        return carry

    lax.fori_loop(0, 4, x_end, 0)


def last_kernel(proj_ref, gate_ref, lat_ref, step_ref, len_ref, vel_ref, adv_ref):
    span = lax.axis_index("span")
    head = lax.axis_index("head")
    level = step_ref[span]
    length = len_ref[span]

    def sigma_of(step):
        fraction = 1.0 - step / STEPS
        return 8.0 * fraction / (1.0 + 7.0 * fraction)

    now = jnp.full((ROWS, 128), level, jnp.int32).astype(F32)
    dt = sigma_of(now + 1.0) - sigma_of(now)
    spot = head * ROWS + lax.broadcasted_iota(jnp.int32, (ROWS, 128), 0)
    live = jnp.where(spot < length, 1.0, 0.0).astype(F32)
    wide = 512
    dt_w = jnp.concatenate([dt] * (wide // 128), axis=1)
    live_w = jnp.concatenate([live] * (wide // 128), axis=1)
    for n in range(D // wide):
        cols = pl.ds(n * wide, wide)
        gate = gate_ref[pl.ds(level, 1), cols]
        vel = (gate * proj_ref[:, cols] * live_w).astype(BF16)
        vel_ref[:, cols] = vel
        adv_ref[:, cols] = lat_ref[:, cols] + dt_w * vel.astype(F32)


def body(query, keys, values, out_weight, time_gates, noise_step, span_length, window_start, latent):
    vmem = pl.BlockSpec(memory_space=pltpu.VMEM)
    smem = pl.BlockSpec(memory_space=pltpu.SMEM)
    dma = pltpu.SemaphoreType.DMA
    projected = pl.pallas_call(
        main_kernel,
        out_shape=jax.ShapeDtypeStruct((ROWS, D), F32),
        in_specs=[vmem, vmem, vmem, vmem, smem, smem],
        out_specs=vmem,
        scratch_shapes=[
            pltpu.VMEM((8, 12 * ROWS, 128), BF16),
            pltpu.VMEM((8, 12 * ROWS, 128), BF16),
            pltpu.VMEM((12, 12 * ROWS, 128), F32),
            pltpu.VMEM((2, NZ, NQ, 128), BF16),
            pltpu.VMEM((4, NQ, 128), BF16),
            pltpu.VMEM((NH, HS, NQ), BF16),
            pltpu.VMEM((NH, HS, NQ), F32),
            pltpu.VMEM((8, 1024), F32),
            pltpu.VMEM((HALF, 128), jnp.int32),
            pltpu.VMEM((2, 8, NQ), jnp.int32),
            pltpu.VMEM((8, 256, CHUNK), BF16),
            pltpu.VMEM((4, NQ, 128), BF16),
            pltpu.VMEM((4, NQ, 128), BF16),
            pltpu.VMEM((4, 8, 256), F32),
            pltpu.VMEM((4, 8, 256), F32),
            pltpu.VMEM((2, HALF, 256), BF16),
            pltpu.VMEM((8, HALF, CHUNK), F32),
            pltpu.VMEM((8, 96, CHUNK), BF16),
            pltpu.VMEM((8, 96, CHUNK), BF16),
            pltpu.VMEM((4, 4, 48, CHUNK), BF16),
            pltpu.VMEM((4, 4, 48, CHUNK), BF16),
            dma((7,)), dma((7,)),
            dma((3,)), dma((3,)),
            dma((2, 2, 8)), dma((2, 2, 8)),
            dma((2, NP)), dma((2, NP)),
            dma((2, NP, 3)), dma((2, NP, 3)),
            dma((3,)), dma((3,)),
            dma((3,)), dma((3,)),
            dma((8,)), dma((8,)),
            dma((4, 3)), dma((4, 3)),
        ],
        compiler_params=pltpu.CompilerParams(
            collective_id=0, has_side_effects=True, vmem_limit_bytes=56 * 1024 * 1024
        ),
        name="attention_tick",
    )(query, keys, values, out_weight, span_length, window_start)
    return pl.pallas_call(
        last_kernel,
        out_shape=(jax.ShapeDtypeStruct((ROWS, D), BF16), jax.ShapeDtypeStruct((ROWS, D), F32)),
        in_specs=[vmem, vmem, vmem, smem, smem],
        out_specs=(vmem, vmem),
        compiler_params=pltpu.CompilerParams(vmem_limit_bytes=32 * 1024 * 1024),
        name="euler_update",
    )(projected, time_gates, latent, noise_step, span_length)


def solution(mesh):
    rows = P(("span", "head"), None)
    return jax.shard_map(
        body,
        mesh=mesh,
        in_specs=(rows, rows, rows, P("head", None), P(), P(), P(), P(), rows),
        out_specs=(rows, rows),
        check_vma=False,
    )
```

```python
import functools
import math

import jax
import jax.numpy as jnp
from jax import lax
from jax.experimental import pallas as pl
from jax.experimental.pallas import tpu as pltpu
from jax.sharding import PartitionSpec as P

MESH = pl.DeviceIdType.MESH
F32 = jnp.float32
BF16 = jnp.bfloat16

D = 5120
HS = 128
STEPS = 30
ROWS = 24
HALF = 192
NQ = 768
NZ = 16
CHUNK = 640
PIECE = 64
NP = 4
TILE = 256
NEG = -1e30
BIG = 3e38
SCALE = math.log2(math.e) / math.sqrt(HS)


def place(x, y, z, core):
    return (y * 8 + z % 8, 4 * x + 2 * (z // 8) + core)


def main_kernel(
    q_ref, k_ref, v_ref, w_ref, slen_ref, wstart_ref, out_ref,
    pack, ex_s, ex_r, stage, send_q, send_kv, kv, vt, qbuf, qt, acc, stat, pos_ref, row_ref, wf,
    robuf, rstat, obuf, send_o, att, fs, send_c, recv_c, send_x, recv_x,
    ex_ss, ex_rs, zq_s, zq_r, zk_s, zk_r, xk_s, xk_r, q_s, q_r, wz_s, wz_r, wy_s, wy_r,
    o_s, o_r, st_s, st_r, a_s, a_r, c_s, c_r, x_s, x_r,
):
    span = lax.axis_index("span")
    head = lax.axis_index("head")
    y, zlo = span // 8, span % 8
    x, zhi, core = head // 4, (head // 2) % 2, head % 2
    z = zhi * 8 + zlo
    quad = z // 4

    def copy(src, dst, ssem, rsem, dev):
        return pltpu.make_async_remote_copy(
            src_ref=src, dst_ref=dst, send_sem=ssem, recv_sem=rsem, device_id=dev, device_id_type=MESH
        )

    def zdev(d):
        return place(x, y, (z + d) % NZ, core)

    def ydev(d):
        return place(x, (y + d) % 4, z, core)

    def xdev(d):
        return place((x + d) % 4, y, z, core)

    twin = place(x, y, z, 1 - core)

    barrier = pltpu.get_barrier_semaphore()

    def greet(dev):
        pl.semaphore_signal(barrier, inc=1, device_id=dev, device_id_type=MESH)

    greet(twin)
    for d in range(1, 4):
        greet(ydev(d))
        greet(xdev(d))

    def greet_z(d, carry):
        greet(zdev(d))
        return carry

    lax.fori_loop(1, NZ, greet_z, 0)

    def greet_o(n, carry):
        sx, sz = n // 4, 4 * x + n % 4

        @pl.when((sx != x) | (sz != z))
        def _():
            greet(place(sx, y, sz, core))

        return carry

    lax.fori_loop(0, NZ, greet_o, 0)

    def pack_tensor(ref, slot):
        def one(n, carry):
            col = 128 * (8 * (n // 4) + 4 * ((n // 2) % 2) + n % 2)
            row = pl.ds(pl.multiple_of(n * ROWS, 8), ROWS)
            theirs = ref[:, pl.ds(pl.multiple_of(col + 256 * (1 - core), 128), 128)]
            pack[row, :] = theirs.astype(F32)
            mine = ref[:, pl.ds(pl.multiple_of(col + 256 * core, 128), 128)]
            stage[slot, pl.ds(pl.multiple_of(n * 48 + core * ROWS, 8), ROWS), :] = mine.astype(F32)
            return carry

        lax.fori_loop(0, NZ, one, 0)
        ex_s[slot] = pack[...].astype(BF16)

    def ex_copy(slot):
        return copy(ex_s.at[slot], ex_r.at[slot], ex_ss.at[slot], ex_rs.at[slot], twin)

    def unpack_tensor(slot):
        ex_copy(slot).wait_recv()
        pack[...] = ex_r[slot].astype(F32)

        def one(n, carry):
            stage[slot, pl.ds(pl.multiple_of(n * 48 + (1 - core) * ROWS, 8), ROWS), :] = pack[
                pl.ds(pl.multiple_of(n * ROWS, 8), ROWS), :
            ]
            return carry

        lax.fori_loop(0, NZ, one, 0)
        return stage[slot].astype(BF16)

    pack_tensor(q_ref, 0)
    pl.semaphore_wait(barrier, 1 + 3 + 3 + 15 + 16 - jnp.where(quad == x, 1, 0))
    ex_copy(0).start()
    pack_tensor(k_ref, 1)
    ex_copy(1).start()
    pack_tensor(v_ref, 2)
    ex_copy(2).start()

    side = (zdev(1), zdev(NZ - 1))

    def wz_forward(direction, i):
        c = 2 * y + direction
        rows = pl.ds(pl.multiple_of(i * PIECE, PIECE), PIECE)
        return copy(
            wf.at[c, rows], wf.at[c, rows], wz_s.at[direction, i], wz_r.at[direction, i], side[direction]
        )

    def wz_origin(direction, i):
        c = 2 * y + direction
        rows = pl.ds(pl.multiple_of(i * PIECE, PIECE), PIECE)
        cols = pl.ds(pl.multiple_of(c * CHUNK, 128), CHUNK)
        return copy(
            w_ref.at[rows, cols], wf.at[c, rows], wz_s.at[direction, i], wz_r.at[direction, i], side[direction]
        )

    def wy_copy(direction, i, d):
        c = 2 * y + direction
        rows = pl.ds(pl.multiple_of(i * PIECE, PIECE), PIECE)
        return copy(
            wf.at[c, rows], wf.at[c, rows], wy_s.at[direction, i, d - 1], wy_r.at[direction, i, d - 1], ydev(d)
        )

    def weight_start():
        for direction in range(2):

            @pl.when(zlo == (7 if direction == 0 else 0))
            def _(direction=direction):
                def go(i, carry):
                    wz_origin(direction, i).start()
                    return carry

                lax.fori_loop(0, NP, go, 0)

    def weight_point(u):
        for direction in range(2):
            hop = zlo if direction == 0 else 7 - zlo
            i = u - hop

            @pl.when((i >= 0) & (i < NP))
            def _(direction=direction, hop=hop, i=i):
                wz_forward(direction, i).wait_recv()

                @pl.when(hop < 7)
                def _():
                    wz_forward(direction, i).start()

                for d in range(1, 4):
                    wy_copy(direction, i, d).start()

    def zrows(n):
        return pl.ds(pl.multiple_of(n * 48, 16), 48)

    def zq_copy(d):
        to = (z + d) % NZ
        return copy(send_q.at[zrows(to)], qbuf.at[y, zrows(z)], zq_s.at[d - 1], zq_r.at[d - 1], zdev(d))

    def zq_in(d):
        src = (z + NZ - d) % NZ
        return copy(send_q.at[zrows(src)], qbuf.at[y, zrows(src)], zq_s.at[d - 1], zq_r.at[d - 1], zdev(d))

    def zk_copy(d):
        to = (z + d) % NZ
        return copy(
            send_kv.at[:, zrows(to)], kv.at[:, z, zrows(x)], zk_s.at[d - 1], zk_r.at[d - 1], zdev(d)
        )

    def zk_in(d):
        src = (z + NZ - d) % NZ
        return copy(
            send_kv.at[:, zrows(src)], kv.at[:, src, zrows(x)], zk_s.at[d - 1], zk_r.at[d - 1], zdev(d)
        )

    def start_both_ways(what):
        def one(t, carry):
            what(t).start()
            what(NZ - t).start()
            return carry

        lax.fori_loop(1, 8, one, 0)
        what(8).start()

    send_q[...] = unpack_tensor(0)
    start_both_ways(zq_copy)
    qbuf[y, zrows(z), :] = send_q[zrows(z), :]
    send_kv[0] = unpack_tensor(1)
    send_kv[1] = unpack_tensor(2)
    start_both_ways(zk_copy)
    for tensor in range(2):
        kv[tensor, z, zrows(x), :] = send_kv[tensor, zrows(z), :]
    weight_start()

    def xk_copy(n, d):
        part = kv.at[:, n, zrows(x)]
        return copy(part, part, xk_s.at[n, d - 1], xk_r.at[n, d - 1], xdev(d))

    def xk_in(n, d):
        part = kv.at[:, n, zrows((x + 4 - d) % 4)]
        return copy(part, part, xk_s.at[n, d - 1], xk_r.at[n, d - 1], xdev(d))

    def spread(n):
        for d in (2, 1, 3):
            xk_copy(n, d).start()

    def spread_pair(t):
        zk_in(t).wait_recv()
        spread((z + NZ - t) % NZ)

        @pl.when(t < 8)
        def _():
            zk_in(NZ - t).wait_recv()
            spread((z + t) % NZ)

    def gathered(n):
        for d in range(1, 4):
            xk_in(n, d).wait_recv()

    spread(z)

    r = lax.broadcasted_iota(jnp.int32, (HALF, 128), 0)
    rx = jnp.where(r >= 48, 1, 0) + jnp.where(r >= 96, 1, 0) + jnp.where(r >= 144, 1, 0)
    pos_ref[...] = r + 48 * rx
    lane = lax.broadcasted_iota(jnp.int32, (8, NQ), 1)
    lz = jnp.zeros((8, NQ), jnp.int32)
    for n in range(1, NZ):
        lz = lz + jnp.where(lane >= 48 * n, 1, 0)
    lz = lz - jnp.where(lz >= 8, 8, 0)
    row_ref[4] = lz

    def first_rows(yy, carry):
        first = jnp.full((8, NQ), wstart_ref[8 * yy], jnp.int32)
        for n in range(1, 8):
            first = jnp.where(lz == n, wstart_ref[8 * yy + n], first)
        row_ref[yy] = first
        stat[yy] = jnp.where(lax.broadcasted_iota(jnp.int32, (8, NQ), 0) < 1, NEG, 0.0).astype(F32)
        acc[yy] = jnp.zeros((HS, NQ), F32)
        return carry

    lax.fori_loop(0, 4, first_rows, 0)

    def zq_wait(d, carry):
        zq_in(d).wait_recv()
        return carry

    lax.fori_loop(1, NZ, zq_wait, 0)

    def q_copy(d):
        return copy(qbuf.at[y], qbuf.at[y], q_s.at[d - 1], q_r.at[d - 1], ydev(4 - d))

    def q_in(d):
        src = (y + d) % 4
        return copy(qbuf.at[src], qbuf.at[src], q_s.at[d - 1], q_r.at[d - 1], ydev(d))

    for d in range(1, 4):

        @pl.when(y - d >= 0)
        def _(d=d):
            q_copy(d).start()

    weight_point(0)
    spread_pair(1)
    weight_point(1)
    spread_pair(2)
    weight_point(2)
    spread_pair(3)

    def turn(yy):
        qt[yy] = qbuf[yy].astype(F32).T.astype(BF16)

    turn(y)
    for d in range(1, 4):

        @pl.when(y + d <= 3)
        def _(d=d):
            q_in(d).wait_recv()
            turn(y + d)

    def blocks(t):
        return (z + NZ - t) % NZ, jnp.where(t == 8, z, (z + t) % NZ)

    def attend(t, low, high):
        sides = []
        for n in blocks(t):
            j = 8 * y + n % 8
            cap = jnp.where(pos_ref[...] + 48 * (n // 8) < slen_ref[j], BIG, NEG).astype(F32)
            sides.append((j, jnp.concatenate([cap, cap], axis=1)))
        za, zb = blocks(t)
        k2 = jnp.concatenate([kv[0, za], kv[0, zb]], axis=0)
        v2 = vt[t - 1]

        def one_row(yy, carry):
            rows = [(row_ref[yy] <= j) & (j <= 8 * yy + row_ref[4]) for j, cap in sides]
            for tile in range(NQ // TILE):
                cols = pl.ds(tile * TILE, TILE)
                s = jnp.dot(k2, qt[yy, :, cols], preferred_element_type=F32) * SCALE
                old = stat[yy, pl.ds(0, 1), cols]
                top = old
                parts = []
                for n in range(2):
                    part = jnp.minimum(s[n * HALF : (n + 1) * HALF], sides[n][1])
                    vis = rows[n][0:1, tile * TILE : (tile + 1) * TILE]
                    top = jnp.maximum(top, jnp.where(vis, jnp.max(part, axis=0, keepdims=True), NEG))
                    parts.append((part, vis))
                factor = jnp.exp2(old - top)
                weight = jnp.concatenate(
                    [jnp.exp2(part - jnp.where(vis, top, BIG)) for part, vis in parts], axis=0
                )
                stat[yy, pl.ds(0, 1), cols] = top
                stat[yy, pl.ds(1, 1), cols] = stat[yy, pl.ds(1, 1), cols] * factor + jnp.sum(
                    weight, axis=0, keepdims=True
                )
                acc[yy, :, cols] = acc[yy, :, cols] * factor + jnp.dot(
                    v2, weight.astype(BF16), preferred_element_type=F32
                )
            return carry

        lax.fori_loop(low, high, one_row, 0)

    def finished(yy):
        return (acc[yy] * (1.0 / jnp.maximum(stat[yy, pl.ds(1, 1), :], 1e-30))).astype(BF16)

    def o_copy(yy, d):
        return (
            copy(stat.at[yy], rstat.at[y], st_s.at[d - 1], st_r.at[d - 1], place(x, yy, z, core)),
            copy(obuf.at[yy], robuf.at[y], o_s.at[d - 1], o_r.at[d - 1], place(x, yy, z, core)),
        )

    def o_in(d):
        src = (y + 4 - d) % 4
        return (
            copy(stat.at[src], rstat.at[src], st_s.at[d - 1], st_r.at[d - 1], ydev(4 - d)),
            copy(obuf.at[src], robuf.at[src], o_s.at[d - 1], o_r.at[d - 1], ydev(4 - d)),
        )

    def give(yy):
        @pl.when(yy == y)
        def _():
            robuf[yy] = finished(yy)
            rstat[yy] = stat[yy]

        for d in range(1, 4):

            @pl.when(y + d == yy)
            def _(d=d):
                obuf[yy] = finished(yy)
                for one in o_copy(yy, d):
                    one.start()

    def first_pass(t, carry):
        @pl.when(t < 6)
        def _():
            spread_pair(t + 3)

        weight_point(2 * t + 1)
        for n in blocks(t):
            gathered(n)
        za, zb = blocks(t)
        vt[t - 1] = jnp.concatenate([kv[1, za], kv[1, zb]], axis=0).T
        attend(t, jnp.maximum(y, 2), 4)
        weight_point(2 * t + 2)
        return carry

    lax.fori_loop(1, 9, first_pass, 0)
    give(3)
    give(2)
    for yy in (1, 0):

        @pl.when(y <= yy)
        def _(yy=yy):
            def one(t, carry):
                attend(t, yy, yy + 1)
                return carry

            lax.fori_loop(1, 9, one, 0)
            give(yy)

    for d in range(1, 4):

        @pl.when(y + d <= 3)
        def _(d=d):
            rstat[y + d] = jnp.where(lax.broadcasted_iota(jnp.int32, (8, NQ), 0) < 1, NEG, 0.0).astype(F32)
            robuf[y + d] = jnp.zeros((HS, NQ), BF16)

        @pl.when(y - d >= 0)
        def _(d=d):
            for one in o_in(d):
                one.wait_recv()

    tops = [rstat[yy, pl.ds(0, 1), :] for yy in range(4)]
    best = jnp.maximum(jnp.maximum(tops[0], tops[1]), jnp.maximum(tops[2], tops[3]))
    shares = [rstat[yy, pl.ds(1, 1), :] * jnp.exp2(tops[yy] - best) for yy in range(4)]
    inv = 1.0 / (shares[0] + shares[1] + shares[2] + shares[3])
    mixed = jnp.zeros((HS, NQ), F32)
    for yy in range(4):
        mixed = mixed + robuf[yy].astype(F32) * (shares[yy] * inv)
    send_o[...] = mixed.T.astype(BF16)

    def a_copy(n):
        return copy(
            send_o.at[zrows(n)], att.at[z % 4, zrows(x)], a_s.at[n], a_r.at[x * 4 + z % 4], place(quad, y, n, core)
        )

    def a_in(n):
        sx = n // 4
        return copy(
            send_o.at[zrows(n)], att.at[n % 4, zrows(sx)], a_s.at[n], a_r.at[n], place(sx, y, 4 * x + n % 4, core)
        )

    def a_send(n, carry):
        to = (z + n) % NZ

        @pl.when((to != z) | (quad != x))
        def _():
            a_copy(to).start()

        return carry

    lax.fori_loop(0, NZ, a_send, 0)

    @pl.when(quad == x)
    def _():
        att[z % 4, zrows(x), :] = send_o[zrows(z), :]

    def wy_wait(n, carry):
        direction, i = n // NP, n % NP
        rows = pl.ds(pl.multiple_of(i * PIECE, PIECE), PIECE)
        for d in range(1, 4):
            c = 2 * ((y + 4 - d) % 4) + direction
            copy(
                wf.at[c, rows], wf.at[c, rows], wy_s.at[direction, i, d - 1], wy_r.at[direction, i, d - 1], ydev(d)
            ).wait_recv()
        return carry

    lax.fori_loop(0, 2 * NP, wy_wait, 0)

    def a_wait(n, carry):
        @pl.when((n // 4 != x) | (4 * x + n % 4 != z))
        def _():
            a_in(n).wait_recv()

        return carry

    lax.fori_loop(0, NZ, a_wait, 0)

    def c_copy(n):
        return copy(send_c.at[n], recv_c.at[n], c_s.at[n], c_r.at[n], twin)

    def core_rows(n, c):
        return jnp.concatenate(
            [fs[n, pl.ds(pl.multiple_of(xx * 48 + c * ROWS, 8), ROWS), :] for xx in range(4)], axis=0
        )

    def project(n):
        cols = pl.ds(pl.multiple_of(n * CHUNK, 128), CHUNK)
        near = jnp.concatenate([att[2 * zhi], att[2 * zhi + 1]], axis=1)
        far = jnp.concatenate([att[2 - 2 * zhi], att[3 - 2 * zhi]], axis=1)
        fs[n] = jnp.dot(near, w_ref[:, cols], preferred_element_type=F32) + jnp.dot(
            far, wf[n], preferred_element_type=F32
        )
        send_c[n] = core_rows(n, 1 - core).astype(BF16)
        c_copy(n).start()

    def x_copy(g, d):
        to = (x + d) % 4
        return copy(
            send_x.at[g, to], recv_x.at[g, x], x_s.at[g, d - 1], x_r.at[g, d - 1], xdev(d)
        )

    def x_in(g, d):
        src = (x + 4 - d) % 4
        return copy(
            send_x.at[g, src], recv_x.at[g, src], x_s.at[g, d - 1], x_r.at[g, d - 1], xdev(d)
        )

    def pair_sum(g):
        parts = []
        for n in range(2):
            c_copy(2 * g + n).wait_recv()
            parts.append(core_rows(2 * g + n, core) + recv_c[2 * g + n].astype(F32))
        for xx in range(4):
            send_x[g, xx] = jnp.concatenate([part[xx * ROWS : (xx + 1) * ROWS] for part in parts], axis=0).astype(BF16)
        for d in (2, 1, 3):
            x_copy(g, d).start()

    def output_step(g, carry):
        @pl.when(g < 4)
        def _():
            project(2 * g)
            project(2 * g + 1)

        @pl.when(g > 0)
        def _():
            pair_sum(g - 1)

        return carry

    lax.fori_loop(0, 5, output_step, 0)

    def collect(g, carry):
        total = send_x[g, x].astype(F32)
        for d in range(1, 4):
            x_in(g, d).wait_recv()
            total = total + recv_x[g, (x + 4 - d) % 4].astype(F32)
        for n in range(2):
            out_ref[:, pl.ds(pl.multiple_of((2 * g + n) * CHUNK, 128), CHUNK)] = total[n * ROWS : (n + 1) * ROWS]
        return carry

    lax.fori_loop(0, 4, collect, 0)

    for slot in range(3):
        ex_copy(slot).wait_send()

    def z_end(d, carry):
        zq_copy(d).wait_send()
        zk_copy(d).wait_send()
        return carry

    lax.fori_loop(1, NZ, z_end, 0)

    def n_end(n, carry):
        for d in range(1, 4):
            xk_copy(n, d).wait_send()

        @pl.when((n != z) | (quad != x))
        def _():
            a_copy(n).wait_send()

        return carry

    lax.fori_loop(0, NZ, n_end, 0)

    def w_end(i, carry):
        for direction in range(2):
            wz_forward(direction, i).wait_send()
            for d in range(1, 4):
                wy_copy(direction, i, d).wait_send()
        return carry

    lax.fori_loop(0, NP, w_end, 0)
    for d in range(1, 4):

        @pl.when(y - d >= 0)
        def _(d=d):
            q_copy(d).wait_send()

        @pl.when(y + d <= 3)
        def _(d=d):
            for one in o_copy(y + d, d):
                one.wait_send()

    def c_end(n, carry):
        c_copy(n).wait_send()
        return carry

    lax.fori_loop(0, 8, c_end, 0)

    def x_end(g, carry):
        for d in range(1, 4):
            x_copy(g, d).wait_send()
        return carry

    lax.fori_loop(0, 4, x_end, 0)


def last_kernel(proj_ref, gate_ref, lat_ref, step_ref, len_ref, vel_ref, adv_ref):
    span = lax.axis_index("span")
    head = lax.axis_index("head")
    level = step_ref[span]
    length = len_ref[span]

    def sigma_of(step):
        fraction = 1.0 - step / STEPS
        return 8.0 * fraction / (1.0 + 7.0 * fraction)

    now = jnp.full((ROWS, 128), level, jnp.int32).astype(F32)
    dt = sigma_of(now + 1.0) - sigma_of(now)
    spot = head * ROWS + lax.broadcasted_iota(jnp.int32, (ROWS, 128), 0)
    live = jnp.where(spot < length, 1.0, 0.0).astype(F32)
    wide = 512
    dt_w = jnp.concatenate([dt] * (wide // 128), axis=1)
    live_w = jnp.concatenate([live] * (wide // 128), axis=1)
    for n in range(D // wide):
        cols = pl.ds(n * wide, wide)
        gate = gate_ref[pl.ds(level, 1), cols]
        vel = (gate * proj_ref[:, cols] * live_w).astype(BF16)
        vel_ref[:, cols] = vel
        adv_ref[:, cols] = lat_ref[:, cols] + dt_w * vel.astype(F32)


def body(query, keys, values, out_weight, time_gates, noise_step, span_length, window_start, latent):
    vmem = pl.BlockSpec(memory_space=pltpu.VMEM)
    smem = pl.BlockSpec(memory_space=pltpu.SMEM)
    dma = pltpu.SemaphoreType.DMA
    projected = pl.pallas_call(
        main_kernel,
        out_shape=jax.ShapeDtypeStruct((ROWS, D), F32),
        in_specs=[vmem, vmem, vmem, vmem, smem, smem],
        out_specs=vmem,
        scratch_shapes=[
            pltpu.VMEM((NZ * ROWS, 128), F32),
            pltpu.VMEM((3, NZ * ROWS, 128), BF16),
            pltpu.VMEM((3, NZ * ROWS, 128), BF16),
            pltpu.VMEM((3, NQ, 128), F32),
            pltpu.VMEM((NQ, 128), BF16),
            pltpu.VMEM((2, NQ, 128), BF16),
            pltpu.VMEM((2, NZ, HALF, 128), BF16),
            pltpu.VMEM((8, HS, 2 * HALF), BF16),
            pltpu.VMEM((4, NQ, 128), BF16),
            pltpu.VMEM((4, HS, NQ), BF16),
            pltpu.VMEM((4, HS, NQ), F32),
            pltpu.VMEM((4, 8, NQ), F32),
            pltpu.VMEM((HALF, 128), jnp.int32),
            pltpu.VMEM((5, 8, NQ), jnp.int32),
            pltpu.VMEM((8, 256, CHUNK), BF16),
            pltpu.VMEM((4, HS, NQ), BF16),
            pltpu.VMEM((4, 8, NQ), F32),
            pltpu.VMEM((4, HS, NQ), BF16),
            pltpu.VMEM((NQ, 128), BF16),
            pltpu.VMEM((4, HALF, 128), BF16),
            pltpu.VMEM((8, HALF, CHUNK), F32),
            pltpu.VMEM((8, 96, CHUNK), BF16),
            pltpu.VMEM((8, 96, CHUNK), BF16),
            pltpu.VMEM((4, 4, 48, CHUNK), BF16),
            pltpu.VMEM((4, 4, 48, CHUNK), BF16),
            dma((3,)), dma((3,)),
            dma((15,)), dma((15,)),
            dma((15,)), dma((15,)),
            dma((NZ, 3)), dma((NZ, 3)),
            dma((3,)), dma((3,)),
            dma((2, NP)), dma((2, NP)),
            dma((2, NP, 3)), dma((2, NP, 3)),
            dma((3,)), dma((3,)),
            dma((3,)), dma((3,)),
            dma((NZ,)), dma((NZ,)),
            dma((8,)), dma((8,)),
            dma((4, 3)), dma((4, 3)),
        ],
        compiler_params=pltpu.CompilerParams(
            collective_id=0, has_side_effects=True, vmem_limit_bytes=40 * 1024 * 1024
        ),
        name="attention_tick",
    )(query, keys, values, out_weight, span_length, window_start)
    return pl.pallas_call(
        last_kernel,
        out_shape=(jax.ShapeDtypeStruct((ROWS, D), BF16), jax.ShapeDtypeStruct((ROWS, D), F32)),
        in_specs=[vmem, vmem, vmem, smem, smem],
        out_specs=(vmem, vmem),
        compiler_params=pltpu.CompilerParams(vmem_limit_bytes=32 * 1024 * 1024),
        name="euler_update",
    )(projected, time_gates, latent, noise_step, span_length)


def solution(mesh):
    rows = P(("span", "head"), None)
    return jax.shard_map(
        body,
        mesh=mesh,
        in_specs=(rows, rows, rows, P("head", None), P(), P(), P(), P(), rows),
        out_specs=(rows, rows),
        check_vma=False,
    )
```

```python
import functools
import math

import jax
import jax.numpy as jnp
from jax import lax
from jax.experimental import pallas as pl
from jax.experimental.pallas import tpu as pltpu
from jax.sharding import PartitionSpec as P

MESH = pl.DeviceIdType.MESH
F32 = jnp.float32
BF16 = jnp.bfloat16

D = 5120
HS = 128
STEPS = 30
ROWS = 24
HALF = 192
NQ = 768
NZ = 16
CHUNK = 640
PIECE = 64
NP = 4
TILE = 256
VT = HS + 16
ACC = HS + 8
NEG = -1e30
BIG = 3e38
SCALE = math.log2(math.e) / math.sqrt(HS)


def place(x, y, z, core):
    return (y * 8 + z % 8, 4 * x + 2 * (z // 8) + core)


def main_kernel(
    q_ref, k_ref, v_ref, w_ref, slen_ref, wstart_ref, out_ref,
    pack, ex_s, ex_r, stage, send_q, send_kv, kv, vt, qbuf, qt, acc, stat, pos_ref, row_ref, wf,
    robuf, rstat, obuf, send_o, att, fs, send_c, recv_c, send_x, recv_x,
    ex_ss, ex_rs, zq_s, zq_r, zk_s, zk_r, xk_s, xk_r, q_s, q_r, wz_s, wz_r, wy_s, wy_r,
    o_s, o_r, st_s, st_r, a_s, a_r, c_s, c_r, x_s, x_r,
):
    span = lax.axis_index("span")
    head = lax.axis_index("head")
    y, zlo = span // 8, span % 8
    x, zhi, core = head // 4, (head // 2) % 2, head % 2
    z = zhi * 8 + zlo
    quad = z // 4

    def copy(src, dst, ssem, rsem, dev):
        return pltpu.make_async_remote_copy(
            src_ref=src, dst_ref=dst, send_sem=ssem, recv_sem=rsem, device_id=dev, device_id_type=MESH
        )

    def zdev(d):
        return place(x, y, (z + d) % NZ, core)

    def ydev(d):
        return place(x, (y + d) % 4, z, core)

    def xdev(d):
        return place((x + d) % 4, y, z, core)

    twin = place(x, y, z, 1 - core)

    barrier = pltpu.get_barrier_semaphore()

    def greet(dev):
        pl.semaphore_signal(barrier, inc=1, device_id=dev, device_id_type=MESH)

    greet(twin)
    for d in range(1, 4):
        greet(ydev(d))
        greet(xdev(d))

    def greet_z(d, carry):
        greet(zdev(d))
        return carry

    lax.fori_loop(1, NZ, greet_z, 0)

    def greet_o(n, carry):
        sx, sz = n // 4, 4 * x + n % 4

        @pl.when((sx != x) | (sz != z))
        def _():
            greet(place(sx, y, sz, core))

        return carry

    lax.fori_loop(0, NZ, greet_o, 0)

    def pack_tensor(ref, slot):
        def one(n, carry):
            col = 128 * (8 * (n // 4) + 4 * ((n // 2) % 2) + n % 2)
            row = pl.ds(pl.multiple_of(n * ROWS, 8), ROWS)
            theirs = ref[:, pl.ds(pl.multiple_of(col + 256 * (1 - core), 128), 128)]
            pack[row, :] = theirs.astype(F32)
            mine = ref[:, pl.ds(pl.multiple_of(col + 256 * core, 128), 128)]
            stage[slot, pl.ds(pl.multiple_of(n * 48 + core * ROWS, 8), ROWS), :] = mine.astype(F32)
            return carry

        lax.fori_loop(0, NZ, one, 0)
        ex_s[slot] = pack[...].astype(BF16)

    def ex_copy(slot):
        return copy(ex_s.at[slot], ex_r.at[slot], ex_ss.at[slot], ex_rs.at[slot], twin)

    def unpack_tensor(slot):
        ex_copy(slot).wait_recv()
        pack[...] = ex_r[slot].astype(F32)

        def one(n, carry):
            stage[slot, pl.ds(pl.multiple_of(n * 48 + (1 - core) * ROWS, 8), ROWS), :] = pack[
                pl.ds(pl.multiple_of(n * ROWS, 8), ROWS), :
            ]
            return carry

        lax.fori_loop(0, NZ, one, 0)
        return stage[slot].astype(BF16)

    pack_tensor(q_ref, 0)
    pl.semaphore_wait(barrier, 1 + 3 + 3 + 15 + 16 - jnp.where(quad == x, 1, 0))
    ex_copy(0).start()
    pack_tensor(k_ref, 1)
    ex_copy(1).start()
    pack_tensor(v_ref, 2)
    ex_copy(2).start()

    side = (zdev(1), zdev(NZ - 1))

    def wz_forward(direction, i):
        c = 2 * y + direction
        rows = pl.ds(pl.multiple_of(i * PIECE, PIECE), PIECE)
        return copy(
            wf.at[c, rows], wf.at[c, rows], wz_s.at[direction, i], wz_r.at[direction, i], side[direction]
        )

    def wz_origin(direction, i):
        c = 2 * y + direction
        rows = pl.ds(pl.multiple_of(i * PIECE, PIECE), PIECE)
        cols = pl.ds(pl.multiple_of(c * CHUNK, 128), CHUNK)
        return copy(
            w_ref.at[rows, cols], wf.at[c, rows], wz_s.at[direction, i], wz_r.at[direction, i], side[direction]
        )

    def wy_copy(direction, i, d):
        c = 2 * y + direction
        rows = pl.ds(pl.multiple_of(i * PIECE, PIECE), PIECE)
        return copy(
            wf.at[c, rows], wf.at[c, rows], wy_s.at[direction, i, d - 1], wy_r.at[direction, i, d - 1], ydev(d)
        )

    def weight_start():
        for direction in range(2):

            @pl.when(zlo == (7 if direction == 0 else 0))
            def _(direction=direction):
                def go(i, carry):
                    wz_origin(direction, i).start()
                    return carry

                lax.fori_loop(0, NP, go, 0)

    def weight_point(u):
        for direction in range(2):
            hop = zlo if direction == 0 else 7 - zlo
            i = u - hop

            @pl.when((i >= 0) & (i < NP))
            def _(direction=direction, hop=hop, i=i):
                wz_forward(direction, i).wait_recv()

                @pl.when(hop < 7)
                def _():
                    wz_forward(direction, i).start()

                for d in range(1, 4):
                    wy_copy(direction, i, d).start()

    def zrows(n):
        return pl.ds(pl.multiple_of(n * 48, 16), 48)

    def zq_copy(d):
        to = (z + d) % NZ
        return copy(send_q.at[zrows(to)], qbuf.at[y, zrows(z)], zq_s.at[d - 1], zq_r.at[d - 1], zdev(d))

    def zq_in(d):
        src = (z + NZ - d) % NZ
        return copy(send_q.at[zrows(src)], qbuf.at[y, zrows(src)], zq_s.at[d - 1], zq_r.at[d - 1], zdev(d))

    def zk_copy(d):
        to = (z + d) % NZ
        return copy(
            send_kv.at[:, zrows(to)], kv.at[:, z, zrows(x)], zk_s.at[d - 1], zk_r.at[d - 1], zdev(d)
        )

    def zk_in(d):
        src = (z + NZ - d) % NZ
        return copy(
            send_kv.at[:, zrows(src)], kv.at[:, src, zrows(x)], zk_s.at[d - 1], zk_r.at[d - 1], zdev(d)
        )

    def start_both_ways(what):
        def one(t, carry):
            what(t).start()
            what(NZ - t).start()
            return carry

        lax.fori_loop(1, 8, one, 0)
        what(8).start()

    send_q[...] = unpack_tensor(0)
    start_both_ways(zq_copy)
    qbuf[y, zrows(z), :] = send_q[zrows(z), :]
    send_kv[0] = unpack_tensor(1)
    send_kv[1] = unpack_tensor(2)
    start_both_ways(zk_copy)
    for tensor in range(2):
        kv[tensor, z, zrows(x), :] = send_kv[tensor, zrows(z), :]
    weight_start()

    def xk_copy(n, d):
        part = kv.at[:, n, zrows(x)]
        return copy(part, part, xk_s.at[n, d - 1], xk_r.at[n, d - 1], xdev(d))

    def xk_in(n, d):
        part = kv.at[:, n, zrows((x + 4 - d) % 4)]
        return copy(part, part, xk_s.at[n, d - 1], xk_r.at[n, d - 1], xdev(d))

    def spread(n):
        for d in (2, 1, 3):
            xk_copy(n, d).start()

    def spread_pair(t):
        zk_in(t).wait_recv()
        spread((z + NZ - t) % NZ)

        @pl.when(t < 8)
        def _():
            zk_in(NZ - t).wait_recv()
            spread((z + t) % NZ)

    def gathered(n):
        for d in range(1, 4):
            xk_in(n, d).wait_recv()

    spread(z)

    r = lax.broadcasted_iota(jnp.int32, (HALF, 128), 0)
    rx = jnp.where(r >= 48, 1, 0) + jnp.where(r >= 96, 1, 0) + jnp.where(r >= 144, 1, 0)
    pos_ref[...] = r + 48 * rx
    lane = lax.broadcasted_iota(jnp.int32, (8, NQ), 1)
    lz = jnp.zeros((8, NQ), jnp.int32)
    for n in range(1, NZ):
        lz = lz + jnp.where(lane >= 48 * n, 1, 0)
    lz = lz - jnp.where(lz >= 8, 8, 0)
    row_ref[4] = lz

    def first_rows(yy, carry):
        first = jnp.full((8, NQ), wstart_ref[8 * yy], jnp.int32)
        for n in range(1, 8):
            first = jnp.where(lz == n, wstart_ref[8 * yy + n], first)
        row_ref[yy] = first
        stat[yy] = jnp.where(lax.broadcasted_iota(jnp.int32, (8, NQ), 0) < 1, NEG, 0.0).astype(F32)
        acc[yy] = jnp.zeros((ACC, NQ), F32)
        return carry

    lax.fori_loop(0, 4, first_rows, 0)

    def zq_wait(d, carry):
        zq_in(d).wait_recv()
        return carry

    lax.fori_loop(1, NZ, zq_wait, 0)

    def q_copy(d):
        return copy(qbuf.at[y], qbuf.at[y], q_s.at[d - 1], q_r.at[d - 1], ydev(4 - d))

    def q_in(d):
        src = (y + d) % 4
        return copy(qbuf.at[src], qbuf.at[src], q_s.at[d - 1], q_r.at[d - 1], ydev(d))

    for d in range(1, 4):

        @pl.when(y - d >= 0)
        def _(d=d):
            q_copy(d).start()

    weight_point(0)
    spread_pair(1)
    weight_point(1)
    spread_pair(2)
    weight_point(2)
    spread_pair(3)

    def turn(yy):
        qt[yy] = qbuf[yy].astype(F32).T.astype(BF16)

    turn(y)

    def blocks(t):
        return (z + NZ - t) % NZ, jnp.where(t == 8, z, (z + t) % NZ)

    def attend(t, low, high):
        sides = []
        for n in blocks(t):
            j = 8 * y + n % 8
            cap = jnp.where(pos_ref[...] + 48 * (n // 8) < slen_ref[j], BIG, NEG).astype(F32)
            sides.append((j, jnp.concatenate([cap, cap], axis=1)))
        za, zb = blocks(t)
        k2 = jnp.concatenate([kv[0, za], kv[0, zb]], axis=0)
        v2 = vt[t - 1]

        def one_row(yy, carry):
            rows = [(row_ref[yy] <= j) & (j <= 8 * yy + row_ref[4]) for j, cap in sides]
            olds = stat[yy, pl.ds(0, 1), :]
            tiles = [slice(n * TILE, (n + 1) * TILE) for n in range(NQ // TILE)]
            scores = [jnp.dot(k2, qt[yy, :, cols], preferred_element_type=F32) for cols in tiles]
            tops, sums = [], []
            for cols, s in zip(tiles, scores):
                top = olds[:, cols]
                parts = []
                for n in range(2):
                    part = jnp.minimum(s[n * HALF : (n + 1) * HALF] * SCALE, sides[n][1])
                    vis = rows[n][0:1, cols]
                    top = jnp.maximum(top, jnp.where(vis, jnp.max(part, axis=0, keepdims=True), NEG))
                    parts.append((part, vis))
                weight = jnp.concatenate(
                    [jnp.exp2(part - jnp.where(vis, top, BIG)).astype(BF16) for part, vis in parts], axis=0
                )
                tops.append(top)
                sums.append(jnp.dot(v2, weight, preferred_element_type=F32))
            for cols, top, part in zip(tiles, tops, sums):
                factor = jnp.exp2(olds[:, cols] - top)
                acc[yy, :, cols] = acc[yy, :, cols] * factor + part[:ACC]
                stat[yy, pl.ds(0, 1), cols] = top
            return carry

        lax.fori_loop(low, high, one_row, 0)

    def finished(yy):
        total = acc[yy, pl.ds(HS, 1), :]
        stat[yy, pl.ds(1, 1), :] = total
        return (acc[yy, pl.ds(0, HS), :] * (1.0 / jnp.maximum(total, 1e-30))).astype(BF16)

    def o_copy(yy, d):
        return (
            copy(stat.at[yy], rstat.at[y], st_s.at[d - 1], st_r.at[d - 1], place(x, yy, z, core)),
            copy(obuf.at[yy], robuf.at[y], o_s.at[d - 1], o_r.at[d - 1], place(x, yy, z, core)),
        )

    def o_in(d):
        src = (y + 4 - d) % 4
        return (
            copy(stat.at[src], rstat.at[src], st_s.at[d - 1], st_r.at[d - 1], ydev(4 - d)),
            copy(obuf.at[src], robuf.at[src], o_s.at[d - 1], o_r.at[d - 1], ydev(4 - d)),
        )

    def give(yy):
        @pl.when(yy == y)
        def _():
            robuf[yy] = finished(yy)
            rstat[yy] = stat[yy]

        for d in range(1, 4):

            @pl.when(y + d == yy)
            def _(d=d):
                obuf[yy] = finished(yy)
                for one in o_copy(yy, d):
                    one.start()

    def first_pass(t, carry):
        @pl.when(t < 6)
        def _():
            spread_pair(t + 3)

        weight_point(2 * t + 1)
        for n in blocks(t):
            gathered(n)
        za, zb = blocks(t)
        vt[t - 1, pl.ds(0, HS), :] = jnp.concatenate([kv[1, za], kv[1, zb]], axis=0).T
        vt[t - 1, pl.ds(HS, VT - HS), :] = jnp.ones((VT - HS, 2 * HALF), BF16)
        attend(t, y, y + 1)
        weight_point(2 * t + 2)
        return carry

    lax.fori_loop(1, 9, first_pass, 0)
    for d in range(1, 4):

        @pl.when(y + d <= 3)
        def _(d=d):
            q_in(d).wait_recv()
            turn(y + d)

    def later_pass(low, high):
        def one(t, carry):
            attend(t, low, high)
            return carry

        lax.fori_loop(1, 9, one, 0)

    later_pass(jnp.maximum(y + 1, 2), 4)
    give(3)
    give(2)

    @pl.when(y == 0)
    def _():
        later_pass(1, 2)

    give(1)
    give(0)
    for d in range(1, 4):

        @pl.when(y + d <= 3)
        def _(d=d):
            rstat[y + d] = jnp.where(lax.broadcasted_iota(jnp.int32, (8, NQ), 0) < 1, NEG, 0.0).astype(F32)
            robuf[y + d] = jnp.zeros((HS, NQ), BF16)

        @pl.when(y - d >= 0)
        def _(d=d):
            for one in o_in(d):
                one.wait_recv()

    tops = [rstat[yy, pl.ds(0, 1), :] for yy in range(4)]
    best = jnp.maximum(jnp.maximum(tops[0], tops[1]), jnp.maximum(tops[2], tops[3]))
    shares = [rstat[yy, pl.ds(1, 1), :] * jnp.exp2(tops[yy] - best) for yy in range(4)]
    inv = 1.0 / (shares[0] + shares[1] + shares[2] + shares[3])
    mixed = jnp.zeros((HS, NQ), F32)
    for yy in range(4):
        mixed = mixed + robuf[yy].astype(F32) * (shares[yy] * inv)
    send_o[...] = mixed.T.astype(BF16)

    def a_copy(n):
        return copy(
            send_o.at[zrows(n)], att.at[z % 4, zrows(x)], a_s.at[n], a_r.at[x * 4 + z % 4], place(quad, y, n, core)
        )

    def a_in(n):
        sx = n // 4
        return copy(
            send_o.at[zrows(n)], att.at[n % 4, zrows(sx)], a_s.at[n], a_r.at[n], place(sx, y, 4 * x + n % 4, core)
        )

    def a_send(n, carry):
        to = (z + n) % NZ

        @pl.when((to != z) | (quad != x))
        def _():
            a_copy(to).start()

        return carry

    lax.fori_loop(0, NZ, a_send, 0)

    @pl.when(quad == x)
    def _():
        att[z % 4, zrows(x), :] = send_o[zrows(z), :]

    def wy_wait(n, carry):
        direction, i = n // NP, n % NP
        rows = pl.ds(pl.multiple_of(i * PIECE, PIECE), PIECE)
        for d in range(1, 4):
            c = 2 * ((y + 4 - d) % 4) + direction
            copy(
                wf.at[c, rows], wf.at[c, rows], wy_s.at[direction, i, d - 1], wy_r.at[direction, i, d - 1], ydev(d)
            ).wait_recv()
        return carry

    lax.fori_loop(0, 2 * NP, wy_wait, 0)

    def a_wait(n, carry):
        @pl.when((n // 4 != x) | (4 * x + n % 4 != z))
        def _():
            a_in(n).wait_recv()

        return carry

    lax.fori_loop(0, NZ, a_wait, 0)

    def c_copy(n):
        return copy(send_c.at[n], recv_c.at[n], c_s.at[n], c_r.at[n], twin)

    def core_rows(n, c):
        return jnp.concatenate(
            [fs[n, pl.ds(pl.multiple_of(xx * 48 + c * ROWS, 8), ROWS), :] for xx in range(4)], axis=0
        )

    def project(n):
        cols = pl.ds(pl.multiple_of(n * CHUNK, 128), CHUNK)
        near = jnp.concatenate([att[2 * zhi], att[2 * zhi + 1]], axis=1)
        far = jnp.concatenate([att[2 - 2 * zhi], att[3 - 2 * zhi]], axis=1)
        fs[n] = jnp.dot(near, w_ref[:, cols], preferred_element_type=F32) + jnp.dot(
            far, wf[n], preferred_element_type=F32
        )
        send_c[n] = core_rows(n, 1 - core).astype(BF16)
        c_copy(n).start()

    def x_copy(g, d):
        to = (x + d) % 4
        return copy(
            send_x.at[g, to], recv_x.at[g, x], x_s.at[g, d - 1], x_r.at[g, d - 1], xdev(d)
        )

    def x_in(g, d):
        src = (x + 4 - d) % 4
        return copy(
            send_x.at[g, src], recv_x.at[g, src], x_s.at[g, d - 1], x_r.at[g, d - 1], xdev(d)
        )

    def pair_sum(g):
        parts = []
        for n in range(2):
            c_copy(2 * g + n).wait_recv()
            parts.append(core_rows(2 * g + n, core) + recv_c[2 * g + n].astype(F32))
        for xx in range(4):
            send_x[g, xx] = jnp.concatenate([part[xx * ROWS : (xx + 1) * ROWS] for part in parts], axis=0).astype(BF16)
        for d in (2, 1, 3):
            x_copy(g, d).start()

    def output_step(g, carry):
        @pl.when(g < 4)
        def _():
            project(2 * g)
            project(2 * g + 1)

        @pl.when(g > 0)
        def _():
            pair_sum(g - 1)

        return carry

    lax.fori_loop(0, 5, output_step, 0)

    def collect(g, carry):
        total = send_x[g, x].astype(F32)
        for d in range(1, 4):
            x_in(g, d).wait_recv()
            total = total + recv_x[g, (x + 4 - d) % 4].astype(F32)
        for n in range(2):
            out_ref[:, pl.ds(pl.multiple_of((2 * g + n) * CHUNK, 128), CHUNK)] = total[n * ROWS : (n + 1) * ROWS]
        return carry

    lax.fori_loop(0, 4, collect, 0)

    for slot in range(3):
        ex_copy(slot).wait_send()

    def z_end(d, carry):
        zq_copy(d).wait_send()
        zk_copy(d).wait_send()
        return carry

    lax.fori_loop(1, NZ, z_end, 0)

    def n_end(n, carry):
        for d in range(1, 4):
            xk_copy(n, d).wait_send()

        @pl.when((n != z) | (quad != x))
        def _():
            a_copy(n).wait_send()

        return carry

    lax.fori_loop(0, NZ, n_end, 0)

    def w_end(i, carry):
        for direction in range(2):
            wz_forward(direction, i).wait_send()
            for d in range(1, 4):
                wy_copy(direction, i, d).wait_send()
        return carry

    lax.fori_loop(0, NP, w_end, 0)
    for d in range(1, 4):

        @pl.when(y - d >= 0)
        def _(d=d):
            q_copy(d).wait_send()

        @pl.when(y + d <= 3)
        def _(d=d):
            for one in o_copy(y + d, d):
                one.wait_send()

    def c_end(n, carry):
        c_copy(n).wait_send()
        return carry

    lax.fori_loop(0, 8, c_end, 0)

    def x_end(g, carry):
        for d in range(1, 4):
            x_copy(g, d).wait_send()
        return carry

    lax.fori_loop(0, 4, x_end, 0)


def last_kernel(proj_ref, gate_ref, lat_ref, step_ref, len_ref, vel_ref, adv_ref):
    span = lax.axis_index("span")
    head = lax.axis_index("head")
    level = step_ref[span]
    length = len_ref[span]

    def sigma_of(step):
        fraction = 1.0 - step / STEPS
        return 8.0 * fraction / (1.0 + 7.0 * fraction)

    now = jnp.full((ROWS, 128), level, jnp.int32).astype(F32)
    dt = sigma_of(now + 1.0) - sigma_of(now)
    spot = head * ROWS + lax.broadcasted_iota(jnp.int32, (ROWS, 128), 0)
    live = jnp.where(spot < length, 1.0, 0.0).astype(F32)
    wide = 512
    dt_w = jnp.concatenate([dt] * (wide // 128), axis=1)
    live_w = jnp.concatenate([live] * (wide // 128), axis=1)
    for n in range(D // wide):
        cols = pl.ds(n * wide, wide)
        gate = gate_ref[pl.ds(level, 1), cols]
        vel = (gate * proj_ref[:, cols] * live_w).astype(BF16)
        vel_ref[:, cols] = vel
        adv_ref[:, cols] = lat_ref[:, cols] + dt_w * vel.astype(F32)


def body(query, keys, values, out_weight, time_gates, noise_step, span_length, window_start, latent):
    vmem = pl.BlockSpec(memory_space=pltpu.VMEM)
    smem = pl.BlockSpec(memory_space=pltpu.SMEM)
    dma = pltpu.SemaphoreType.DMA
    projected = pl.pallas_call(
        main_kernel,
        out_shape=jax.ShapeDtypeStruct((ROWS, D), F32),
        in_specs=[vmem, vmem, vmem, vmem, smem, smem],
        out_specs=vmem,
        scratch_shapes=[
            pltpu.VMEM((NZ * ROWS, 128), F32),
            pltpu.VMEM((3, NZ * ROWS, 128), BF16),
            pltpu.VMEM((3, NZ * ROWS, 128), BF16),
            pltpu.VMEM((3, NQ, 128), F32),
            pltpu.VMEM((NQ, 128), BF16),
            pltpu.VMEM((2, NQ, 128), BF16),
            pltpu.VMEM((2, NZ, HALF, 128), BF16),
            pltpu.VMEM((8, VT, 2 * HALF), BF16),
            pltpu.VMEM((4, NQ, 128), BF16),
            pltpu.VMEM((4, HS, NQ), BF16),
            pltpu.VMEM((4, ACC, NQ), F32),
            pltpu.VMEM((4, 8, NQ), F32),
            pltpu.VMEM((HALF, 128), jnp.int32),
            pltpu.VMEM((5, 8, NQ), jnp.int32),
            pltpu.VMEM((8, 256, CHUNK), BF16),
            pltpu.VMEM((4, HS, NQ), BF16),
            pltpu.VMEM((4, 8, NQ), F32),
            pltpu.VMEM((4, HS, NQ), BF16),
            pltpu.VMEM((NQ, 128), BF16),
            pltpu.VMEM((4, HALF, 128), BF16),
            pltpu.VMEM((8, HALF, CHUNK), F32),
            pltpu.VMEM((8, 96, CHUNK), BF16),
            pltpu.VMEM((8, 96, CHUNK), BF16),
            pltpu.VMEM((4, 4, 48, CHUNK), BF16),
            pltpu.VMEM((4, 4, 48, CHUNK), BF16),
            dma((3,)), dma((3,)),
            dma((15,)), dma((15,)),
            dma((15,)), dma((15,)),
            dma((NZ, 3)), dma((NZ, 3)),
            dma((3,)), dma((3,)),
            dma((2, NP)), dma((2, NP)),
            dma((2, NP, 3)), dma((2, NP, 3)),
            dma((3,)), dma((3,)),
            dma((3,)), dma((3,)),
            dma((NZ,)), dma((NZ,)),
            dma((8,)), dma((8,)),
            dma((4, 3)), dma((4, 3)),
        ],
        compiler_params=pltpu.CompilerParams(
            collective_id=0, has_side_effects=True, vmem_limit_bytes=40 * 1024 * 1024
        ),
        name="attention_tick",
    )(query, keys, values, out_weight, span_length, window_start)
    return pl.pallas_call(
        last_kernel,
        out_shape=(jax.ShapeDtypeStruct((ROWS, D), BF16), jax.ShapeDtypeStruct((ROWS, D), F32)),
        in_specs=[vmem, vmem, vmem, smem, smem],
        out_specs=(vmem, vmem),
        compiler_params=pltpu.CompilerParams(vmem_limit_bytes=32 * 1024 * 1024),
        name="euler_update",
    )(projected, time_gates, latent, noise_step, span_length)


def solution(mesh):
    rows = P(("span", "head"), None)
    return jax.shard_map(
        body,
        mesh=mesh,
        in_specs=(rows, rows, rows, P("head", None), P(), P(), P(), P(), rows),
        out_specs=(rows, rows),
        check_vma=False,
    )
```

```python
import functools
import math

import jax
import jax.numpy as jnp
from jax import lax
from jax.experimental import pallas as pl
from jax.experimental.pallas import tpu as pltpu
from jax.sharding import PartitionSpec as P

MESH = pl.DeviceIdType.MESH
F32 = jnp.float32
BF16 = jnp.bfloat16

D = 5120
HS = 128
STEPS = 30
ROWS = 24
HALF = 192
NQ = 768
NZ = 16
CHUNK = 640
PIECE = 64
NP = 4
TILE = 256
VT = HS + 16
ACC = HS + 8
NEG = -1e30
BIG = 3e38
SCALE = math.log2(math.e) / math.sqrt(HS)


def place(x, y, z, core):
    return (y * 8 + z % 8, 4 * x + 2 * (z // 8) + core)


def main_kernel(
    q_ref, k_ref, v_ref, w_hbm, slen_ref, wstart_ref, out_ref,
    w_ref, w_sem, pack, ex_s, ex_r, stage, send_q, send_kv, kv, vt, qbuf, qt, acc, stat, pos_ref, row_ref, wf,
    robuf, rstat, obuf, send_o, att, fs, send_c, recv_c, send_x, recv_x,
    ex_ss, ex_rs, zq_s, zq_r, zk_s, zk_r, xk_s, xk_r, q_s, q_r, wz_s, wz_r, wy_s, wy_r,
    o_s, o_r, st_s, st_r, a_s, a_r, c_s, c_r, x_s, x_r,
):
    span = lax.axis_index("span")
    head = lax.axis_index("head")
    y, zlo = span // 8, span % 8
    x, zhi, core = head // 4, (head // 2) % 2, head % 2
    z = zhi * 8 + zlo
    quad = z // 4

    def copy(src, dst, ssem, rsem, dev):
        return pltpu.make_async_remote_copy(
            src_ref=src, dst_ref=dst, send_sem=ssem, recv_sem=rsem, device_id=dev, device_id_type=MESH
        )

    def zdev(d):
        return place(x, y, (z + d) % NZ, core)

    def ydev(d):
        return place(x, (y + d) % 4, z, core)

    def xdev(d):
        return place((x + d) % 4, y, z, core)

    twin = place(x, y, z, 1 - core)

    barrier = pltpu.get_barrier_semaphore()

    def greet(dev):
        pl.semaphore_signal(barrier, inc=1, device_id=dev, device_id_type=MESH)

    greet(twin)
    for d in range(1, 4):
        greet(ydev(d))
        greet(xdev(d))

    def greet_z(d, carry):
        greet(zdev(d))
        return carry

    lax.fori_loop(1, NZ, greet_z, 0)

    def greet_o(n, carry):
        sx, sz = n // 4, 4 * x + n % 4

        @pl.when((sx != x) | (sz != z))
        def _():
            greet(place(sx, y, sz, core))

        return carry

    lax.fori_loop(0, NZ, greet_o, 0)

    def pack_tensor(ref, slot):
        def one(n, carry):
            col = 128 * (8 * (n // 4) + 4 * ((n // 2) % 2) + n % 2)
            row = pl.ds(pl.multiple_of(n * ROWS, 8), ROWS)
            theirs = ref[:, pl.ds(pl.multiple_of(col + 256 * (1 - core), 128), 128)]
            pack[row, :] = theirs.astype(F32)
            mine = ref[:, pl.ds(pl.multiple_of(col + 256 * core, 128), 128)]
            stage[slot, pl.ds(pl.multiple_of(n * 48 + core * ROWS, 8), ROWS), :] = mine.astype(F32)
            return carry

        lax.fori_loop(0, NZ, one, 0)
        ex_s[slot] = pack[...].astype(BF16)

    def ex_copy(slot):
        return copy(ex_s.at[slot], ex_r.at[slot], ex_ss.at[slot], ex_rs.at[slot], twin)

    def unpack_tensor(slot):
        ex_copy(slot).wait_recv()
        pack[...] = ex_r[slot].astype(F32)

        def one(n, carry):
            stage[slot, pl.ds(pl.multiple_of(n * 48 + (1 - core) * ROWS, 8), ROWS), :] = pack[
                pl.ds(pl.multiple_of(n * ROWS, 8), ROWS), :
            ]
            return carry

        lax.fori_loop(0, NZ, one, 0)
        return stage[slot].astype(BF16)

    side = (zdev(1), zdev(NZ - 1))

    def wz_forward(direction, i):
        c = 2 * y + direction
        rows = pl.ds(pl.multiple_of(i * PIECE, PIECE), PIECE)
        return copy(
            wf.at[c, rows], wf.at[c, rows], wz_s.at[direction, i], wz_r.at[direction, i], side[direction]
        )

    def wz_origin(direction, i):
        c = 2 * y + direction
        rows = pl.ds(pl.multiple_of(i * PIECE, PIECE), PIECE)
        cols = pl.ds(pl.multiple_of(c * CHUNK, 128), CHUNK)
        return copy(
            w_hbm.at[rows, cols], wf.at[c, rows], wz_s.at[direction, i], wz_r.at[direction, i], side[direction]
        )

    def wy_copy(direction, i, d):
        c = 2 * y + direction
        rows = pl.ds(pl.multiple_of(i * PIECE, PIECE), PIECE)
        return copy(
            wf.at[c, rows], wf.at[c, rows], wy_s.at[direction, i, d - 1], wy_r.at[direction, i, d - 1], ydev(d)
        )

    def weight_start():
        for direction in range(2):

            @pl.when(zlo == (7 if direction == 0 else 0))
            def _(direction=direction):
                def go(i, carry):
                    wz_origin(direction, i).start()
                    return carry

                lax.fori_loop(0, NP, go, 0)

    def weight_point(u):
        for direction in range(2):
            hop = zlo if direction == 0 else 7 - zlo
            i = u - hop

            @pl.when((i >= 0) & (i < NP))
            def _(direction=direction, hop=hop, i=i):
                wz_forward(direction, i).wait_recv()

                @pl.when(hop < 7)
                def _():
                    wz_forward(direction, i).start()

                for d in range(1, 4):
                    wy_copy(direction, i, d).start()

    own_weight = pltpu.make_async_copy(w_hbm, w_ref, w_sem)
    own_weight.start()
    pack_tensor(q_ref, 0)
    pl.semaphore_wait(barrier, 1 + 3 + 3 + 15 + 16 - jnp.where(quad == x, 1, 0))
    ex_copy(0).start()
    weight_start()
    pack_tensor(k_ref, 1)
    ex_copy(1).start()
    pack_tensor(v_ref, 2)
    ex_copy(2).start()

    def zrows(n):
        return pl.ds(pl.multiple_of(n * 48, 16), 48)

    def zq_copy(d):
        to = (z + d) % NZ
        return copy(send_q.at[zrows(to)], qbuf.at[y, zrows(z)], zq_s.at[d - 1], zq_r.at[d - 1], zdev(d))

    def zq_in(d):
        src = (z + NZ - d) % NZ
        return copy(send_q.at[zrows(src)], qbuf.at[y, zrows(src)], zq_s.at[d - 1], zq_r.at[d - 1], zdev(d))

    def zk_copy(d):
        to = (z + d) % NZ
        return copy(
            send_kv.at[:, zrows(to)], kv.at[:, z, zrows(x)], zk_s.at[d - 1], zk_r.at[d - 1], zdev(d)
        )

    def zk_in(d):
        src = (z + NZ - d) % NZ
        return copy(
            send_kv.at[:, zrows(src)], kv.at[:, src, zrows(x)], zk_s.at[d - 1], zk_r.at[d - 1], zdev(d)
        )

    def start_both_ways(what):
        def one(t, carry):
            what(t).start()
            what(NZ - t).start()
            return carry

        lax.fori_loop(1, 8, one, 0)
        what(8).start()

    send_q[...] = unpack_tensor(0)
    start_both_ways(zq_copy)
    qbuf[y, zrows(z), :] = send_q[zrows(z), :]
    send_kv[0] = unpack_tensor(1)
    send_kv[1] = unpack_tensor(2)
    start_both_ways(zk_copy)
    weight_point(0)
    for tensor in range(2):
        kv[tensor, z, zrows(x), :] = send_kv[tensor, zrows(z), :]

    def xk_copy(n, d):
        part = kv.at[:, n, zrows(x)]
        return copy(part, part, xk_s.at[n, d - 1], xk_r.at[n, d - 1], xdev(d))

    def xk_in(n, d):
        part = kv.at[:, n, zrows((x + 4 - d) % 4)]
        return copy(part, part, xk_s.at[n, d - 1], xk_r.at[n, d - 1], xdev(d))

    def spread(n):
        for d in (2, 1, 3):
            xk_copy(n, d).start()

    def spread_pair(t):
        zk_in(t).wait_recv()
        spread((z + NZ - t) % NZ)

        @pl.when(t < 8)
        def _():
            zk_in(NZ - t).wait_recv()
            spread((z + t) % NZ)

    def gathered(n):
        for d in range(1, 4):
            xk_in(n, d).wait_recv()

    spread(z)

    r = lax.broadcasted_iota(jnp.int32, (HALF, 128), 0)
    rx = jnp.where(r >= 48, 1, 0) + jnp.where(r >= 96, 1, 0) + jnp.where(r >= 144, 1, 0)
    pos_ref[...] = r + 48 * rx
    lane = lax.broadcasted_iota(jnp.int32, (8, NQ), 1)
    lz = jnp.zeros((8, NQ), jnp.int32)
    for n in range(1, NZ):
        lz = lz + jnp.where(lane >= 48 * n, 1, 0)
    lz = lz - jnp.where(lz >= 8, 8, 0)
    row_ref[4] = lz

    def first_rows(yy, carry):
        first = jnp.full((8, NQ), wstart_ref[8 * yy], jnp.int32)
        for n in range(1, 8):
            first = jnp.where(lz == n, wstart_ref[8 * yy + n], first)
        row_ref[yy] = first
        stat[yy] = jnp.where(lax.broadcasted_iota(jnp.int32, (8, NQ), 0) < 1, NEG, 0.0).astype(F32)
        acc[yy] = jnp.zeros((ACC, NQ), F32)
        return carry

    lax.fori_loop(0, 4, first_rows, 0)

    def zq_wait(d, carry):
        zq_in(d).wait_recv()
        return carry

    lax.fori_loop(1, NZ, zq_wait, 0)

    def q_copy(d):
        return copy(qbuf.at[y], qbuf.at[y], q_s.at[d - 1], q_r.at[d - 1], ydev(4 - d))

    def q_in(d):
        src = (y + d) % 4
        return copy(qbuf.at[src], qbuf.at[src], q_s.at[d - 1], q_r.at[d - 1], ydev(d))

    for d in range(1, 4):

        @pl.when(y - d >= 0)
        def _(d=d):
            q_copy(d).start()

    weight_point(1)
    spread_pair(1)
    spread_pair(2)
    weight_point(2)
    spread_pair(3)

    def turn(yy):
        qt[yy] = qbuf[yy].astype(F32).T.astype(BF16)

    turn(y)

    def blocks(t):
        return (z + NZ - t) % NZ, jnp.where(t == 8, z, (z + t) % NZ)

    def attend(t, low, high):
        sides = []
        for n in blocks(t):
            j = 8 * y + n % 8
            cap = jnp.where(pos_ref[...] + 48 * (n // 8) < slen_ref[j], BIG, NEG).astype(F32)
            sides.append((j, jnp.concatenate([cap, cap], axis=1)))
        za, zb = blocks(t)
        k2 = jnp.concatenate([kv[0, za], kv[0, zb]], axis=0)
        v2 = vt[t - 1]

        def one_row(yy, carry):
            rows = [(row_ref[yy] <= j) & (j <= 8 * yy + row_ref[4]) for j, cap in sides]
            olds = stat[yy, pl.ds(0, 1), :]
            tiles = [slice(n * TILE, (n + 1) * TILE) for n in range(NQ // TILE)]
            scores = [jnp.dot(k2, qt[yy, :, cols], preferred_element_type=F32) for cols in tiles]
            tops, sums = [], []
            for cols, s in zip(tiles, scores):
                top = olds[:, cols]
                parts = []
                for n in range(2):
                    part = jnp.minimum(s[n * HALF : (n + 1) * HALF] * SCALE, sides[n][1])
                    vis = rows[n][0:1, cols]
                    top = jnp.maximum(top, jnp.where(vis, jnp.max(part, axis=0, keepdims=True), NEG))
                    parts.append((part, vis))
                weight = jnp.concatenate(
                    [jnp.exp2(part - jnp.where(vis, top, BIG)).astype(BF16) for part, vis in parts], axis=0
                )
                tops.append(top)
                sums.append(jnp.dot(v2, weight, preferred_element_type=F32))
            for cols, top, part in zip(tiles, tops, sums):
                factor = jnp.exp2(olds[:, cols] - top)
                acc[yy, :, cols] = acc[yy, :, cols] * factor + part[:ACC]
                stat[yy, pl.ds(0, 1), cols] = top
            return carry

        lax.fori_loop(low, high, one_row, 0)

    def finished(yy):
        total = acc[yy, pl.ds(HS, 1), :]
        stat[yy, pl.ds(1, 1), :] = total
        return (acc[yy, pl.ds(0, HS), :] * (1.0 / jnp.maximum(total, 1e-30))).astype(BF16)

    def o_copy(yy, d):
        return (
            copy(stat.at[yy], rstat.at[y], st_s.at[d - 1], st_r.at[d - 1], place(x, yy, z, core)),
            copy(obuf.at[yy], robuf.at[y], o_s.at[d - 1], o_r.at[d - 1], place(x, yy, z, core)),
        )

    def o_in(d):
        src = (y + 4 - d) % 4
        return (
            copy(stat.at[src], rstat.at[src], st_s.at[d - 1], st_r.at[d - 1], ydev(4 - d)),
            copy(obuf.at[src], robuf.at[src], o_s.at[d - 1], o_r.at[d - 1], ydev(4 - d)),
        )

    def give(yy):
        @pl.when(yy == y)
        def _():
            robuf[yy] = finished(yy)
            rstat[yy] = stat[yy]

        for d in range(1, 4):

            @pl.when(y + d == yy)
            def _(d=d):
                obuf[yy] = finished(yy)
                for one in o_copy(yy, d):
                    one.start()

    def first_pass(t, carry):
        @pl.when(t < 6)
        def _():
            spread_pair(t + 3)

        for n in blocks(t):
            gathered(n)
        za, zb = blocks(t)
        vt[t - 1, pl.ds(0, HS), :] = jnp.concatenate([kv[1, za], kv[1, zb]], axis=0).T
        vt[t - 1, pl.ds(HS, VT - HS), :] = jnp.ones((VT - HS, 2 * HALF), BF16)
        attend(t, y, y + 1)
        weight_point(t + 2)
        return carry

    lax.fori_loop(1, 9, first_pass, 0)
    for d in range(1, 4):

        @pl.when(y + d <= 3)
        def _(d=d):
            q_in(d).wait_recv()
            turn(y + d)

    def later_pass(low, high):
        def one(t, carry):
            attend(t, low, high)
            return carry

        lax.fori_loop(1, 9, one, 0)

    later_pass(jnp.maximum(y + 1, 2), 4)
    give(3)
    give(2)

    @pl.when(y == 0)
    def _():
        later_pass(1, 2)

    give(1)
    give(0)
    for d in range(1, 4):

        @pl.when(y + d <= 3)
        def _(d=d):
            rstat[y + d] = jnp.where(lax.broadcasted_iota(jnp.int32, (8, NQ), 0) < 1, NEG, 0.0).astype(F32)
            robuf[y + d] = jnp.zeros((HS, NQ), BF16)

        @pl.when(y - d >= 0)
        def _(d=d):
            for one in o_in(d):
                one.wait_recv()

    tops = [rstat[yy, pl.ds(0, 1), :] for yy in range(4)]
    best = jnp.maximum(jnp.maximum(tops[0], tops[1]), jnp.maximum(tops[2], tops[3]))
    shares = [rstat[yy, pl.ds(1, 1), :] * jnp.exp2(tops[yy] - best) for yy in range(4)]
    inv = 1.0 / (shares[0] + shares[1] + shares[2] + shares[3])
    mixed = jnp.zeros((HS, NQ), F32)
    for yy in range(4):
        mixed = mixed + robuf[yy].astype(F32) * (shares[yy] * inv)
    send_o[...] = mixed.T.astype(BF16)

    def a_copy(n):
        return copy(
            send_o.at[zrows(n)], att.at[z % 4, zrows(x)], a_s.at[n], a_r.at[x * 4 + z % 4], place(quad, y, n, core)
        )

    def a_in(n):
        sx = n // 4
        return copy(
            send_o.at[zrows(n)], att.at[n % 4, zrows(sx)], a_s.at[n], a_r.at[n], place(sx, y, 4 * x + n % 4, core)
        )

    def a_send(n, carry):
        to = (z + n) % NZ

        @pl.when((to != z) | (quad != x))
        def _():
            a_copy(to).start()

        return carry

    lax.fori_loop(0, NZ, a_send, 0)

    @pl.when(quad == x)
    def _():
        att[z % 4, zrows(x), :] = send_o[zrows(z), :]

    for slot in range(3):
        ex_copy(slot).wait_send()

    def z_end(d, carry):
        zq_copy(d).wait_send()
        zk_copy(d).wait_send()
        return carry

    lax.fori_loop(1, NZ, z_end, 0)

    def n_end(n, carry):
        for d in range(1, 4):
            xk_copy(n, d).wait_send()

        return carry

    lax.fori_loop(0, NZ, n_end, 0)

    def w_end(i, carry):
        for direction in range(2):
            wz_forward(direction, i).wait_send()
            for d in range(1, 4):
                wy_copy(direction, i, d).wait_send()
        return carry

    lax.fori_loop(0, NP, w_end, 0)
    for d in range(1, 4):

        @pl.when(y - d >= 0)
        def _(d=d):
            q_copy(d).wait_send()

        @pl.when(y + d <= 3)
        def _(d=d):
            for one in o_copy(y + d, d):
                one.wait_send()

    own_weight.wait()

    def wy_wait(n, carry):
        direction, i = n // NP, n % NP
        rows = pl.ds(pl.multiple_of(i * PIECE, PIECE), PIECE)
        for d in range(1, 4):
            c = 2 * ((y + 4 - d) % 4) + direction
            copy(
                wf.at[c, rows], wf.at[c, rows], wy_s.at[direction, i, d - 1], wy_r.at[direction, i, d - 1], ydev(d)
            ).wait_recv()
        return carry

    lax.fori_loop(0, 2 * NP, wy_wait, 0)

    def a_wait(n, carry):
        @pl.when((n // 4 != x) | (4 * x + n % 4 != z))
        def _():
            a_in(n).wait_recv()

        return carry

    lax.fori_loop(0, NZ, a_wait, 0)

    def c_copy(n):
        return copy(send_c.at[n], recv_c.at[n], c_s.at[n], c_r.at[n], twin)

    def core_rows(n, c):
        return jnp.concatenate(
            [fs[n, pl.ds(pl.multiple_of(xx * 48 + c * ROWS, 8), ROWS), :] for xx in range(4)], axis=0
        )

    def project(n):
        cols = pl.ds(pl.multiple_of(n * CHUNK, 128), CHUNK)
        near = jnp.concatenate([att[2 * zhi], att[2 * zhi + 1]], axis=1)
        far = jnp.concatenate([att[2 - 2 * zhi], att[3 - 2 * zhi]], axis=1)
        fs[n] = jnp.dot(near, w_ref[:, cols], preferred_element_type=F32) + jnp.dot(
            far, wf[n], preferred_element_type=F32
        )
        send_c[n] = core_rows(n, 1 - core).astype(BF16)
        c_copy(n).start()

    def x_copy(g, d):
        to = (x + d) % 4
        return copy(
            send_x.at[g, to], recv_x.at[g, x], x_s.at[g, d - 1], x_r.at[g, d - 1], xdev(d)
        )

    def x_in(g, d):
        src = (x + 4 - d) % 4
        return copy(
            send_x.at[g, src], recv_x.at[g, src], x_s.at[g, d - 1], x_r.at[g, d - 1], xdev(d)
        )

    def pair_sum(g):
        parts = []
        for n in range(2):
            c_copy(2 * g + n).wait_recv()
            parts.append(core_rows(2 * g + n, core) + recv_c[2 * g + n].astype(F32))
        for xx in range(4):
            send_x[g, xx] = jnp.concatenate([part[xx * ROWS : (xx + 1) * ROWS] for part in parts], axis=0).astype(BF16)
        for d in (2, 1, 3):
            x_copy(g, d).start()

    def output_step(g, carry):
        @pl.when(g < 4)
        def _():
            project(2 * g)
            project(2 * g + 1)

        @pl.when(g > 0)
        def _():
            pair_sum(g - 1)

        return carry

    lax.fori_loop(0, 5, output_step, 0)

    def collect(g, carry):
        total = send_x[g, x].astype(F32)
        for d in range(1, 4):
            x_in(g, d).wait_recv()
            total = total + recv_x[g, (x + 4 - d) % 4].astype(F32)
        for n in range(2):
            out_ref[:, pl.ds(pl.multiple_of((2 * g + n) * CHUNK, 128), CHUNK)] = total[n * ROWS : (n + 1) * ROWS]
        return carry

    lax.fori_loop(0, 4, collect, 0)

    def c_end(n, carry):
        c_copy(n).wait_send()
        return carry

    lax.fori_loop(0, 8, c_end, 0)

    def a_end(n, carry):
        @pl.when((n != z) | (quad != x))
        def _():
            a_copy(n).wait_send()

        return carry

    lax.fori_loop(0, NZ, a_end, 0)

    def x_end(g, carry):
        for d in range(1, 4):
            x_copy(g, d).wait_send()
        return carry

    lax.fori_loop(0, 4, x_end, 0)


def last_kernel(proj_ref, gate_ref, lat_ref, step_ref, len_ref, vel_ref, adv_ref):
    span = lax.axis_index("span")
    head = lax.axis_index("head")
    level = step_ref[span]
    length = len_ref[span]

    def sigma_of(step):
        fraction = 1.0 - step / STEPS
        return 8.0 * fraction / (1.0 + 7.0 * fraction)

    now = jnp.full((ROWS, 128), level, jnp.int32).astype(F32)
    dt = sigma_of(now + 1.0) - sigma_of(now)
    spot = head * ROWS + lax.broadcasted_iota(jnp.int32, (ROWS, 128), 0)
    live = jnp.where(spot < length, 1.0, 0.0).astype(F32)
    wide = 512
    dt_w = jnp.concatenate([dt] * (wide // 128), axis=1)
    live_w = jnp.concatenate([live] * (wide // 128), axis=1)
    for n in range(D // wide):
        cols = pl.ds(n * wide, wide)
        gate = gate_ref[pl.ds(level, 1), cols]
        vel = (gate * proj_ref[:, cols] * live_w).astype(BF16)
        vel_ref[:, cols] = vel
        adv_ref[:, cols] = lat_ref[:, cols] + dt_w * vel.astype(F32)


def body(query, keys, values, out_weight, time_gates, noise_step, span_length, window_start, latent):
    vmem = pl.BlockSpec(memory_space=pltpu.VMEM)
    smem = pl.BlockSpec(memory_space=pltpu.SMEM)
    dma = pltpu.SemaphoreType.DMA
    projected = pl.pallas_call(
        main_kernel,
        out_shape=jax.ShapeDtypeStruct((ROWS, D), F32),
        in_specs=[vmem, vmem, vmem, pl.BlockSpec(memory_space=pl.ANY), smem, smem],
        out_specs=vmem,
        scratch_shapes=[
            pltpu.VMEM((256, D), BF16),
            dma,
            pltpu.VMEM((NZ * ROWS, 128), F32),
            pltpu.VMEM((3, NZ * ROWS, 128), BF16),
            pltpu.VMEM((3, NZ * ROWS, 128), BF16),
            pltpu.VMEM((3, NQ, 128), F32),
            pltpu.VMEM((NQ, 128), BF16),
            pltpu.VMEM((2, NQ, 128), BF16),
            pltpu.VMEM((2, NZ, HALF, 128), BF16),
            pltpu.VMEM((8, VT, 2 * HALF), BF16),
            pltpu.VMEM((4, NQ, 128), BF16),
            pltpu.VMEM((4, HS, NQ), BF16),
            pltpu.VMEM((4, ACC, NQ), F32),
            pltpu.VMEM((4, 8, NQ), F32),
            pltpu.VMEM((HALF, 128), jnp.int32),
            pltpu.VMEM((5, 8, NQ), jnp.int32),
            pltpu.VMEM((8, 256, CHUNK), BF16),
            pltpu.VMEM((4, HS, NQ), BF16),
            pltpu.VMEM((4, 8, NQ), F32),
            pltpu.VMEM((4, HS, NQ), BF16),
            pltpu.VMEM((NQ, 128), BF16),
            pltpu.VMEM((4, HALF, 128), BF16),
            pltpu.VMEM((8, HALF, CHUNK), F32),
            pltpu.VMEM((8, 96, CHUNK), BF16),
            pltpu.VMEM((8, 96, CHUNK), BF16),
            pltpu.VMEM((4, 4, 48, CHUNK), BF16),
            pltpu.VMEM((4, 4, 48, CHUNK), BF16),
            dma((3,)), dma((3,)),
            dma((15,)), dma((15,)),
            dma((15,)), dma((15,)),
            dma((NZ, 3)), dma((NZ, 3)),
            dma((3,)), dma((3,)),
            dma((2, NP)), dma((2, NP)),
            dma((2, NP, 3)), dma((2, NP, 3)),
            dma((3,)), dma((3,)),
            dma((3,)), dma((3,)),
            dma((NZ,)), dma((NZ,)),
            dma((8,)), dma((8,)),
            dma((4, 3)), dma((4, 3)),
        ],
        compiler_params=pltpu.CompilerParams(
            collective_id=0, has_side_effects=True, vmem_limit_bytes=40 * 1024 * 1024
        ),
        name="attention_tick",
    )(query, keys, values, out_weight, span_length, window_start)
    return pl.pallas_call(
        last_kernel,
        out_shape=(jax.ShapeDtypeStruct((ROWS, D), BF16), jax.ShapeDtypeStruct((ROWS, D), F32)),
        in_specs=[vmem, vmem, vmem, smem, smem],
        out_specs=(vmem, vmem),
        compiler_params=pltpu.CompilerParams(vmem_limit_bytes=32 * 1024 * 1024),
        name="euler_update",
    )(projected, time_gates, latent, noise_step, span_length)


def solution(mesh):
    rows = P(("span", "head"), None)
    return jax.shard_map(
        body,
        mesh=mesh,
        in_specs=(rows, rows, rows, P("head", None), P(), P(), P(), P(), rows),
        out_specs=(rows, rows),
        check_vma=False,
    )
```

```python
import functools
import math

import jax
import jax.numpy as jnp
from jax import lax
from jax.experimental import pallas as pl
from jax.experimental.pallas import tpu as pltpu
from jax.sharding import PartitionSpec as P

MESH = pl.DeviceIdType.MESH
F32 = jnp.float32
BF16 = jnp.bfloat16

D = 5120
HS = 128
STEPS = 30
ROWS = 24
HALF = 192
NQ = 768
NZ = 16
CHUNK = 640
PIECE = 64
NP = 4
EARLY = 3
TILE = 256
VT = HS + 16
ACC = HS + 8
NEG = -1e30
BIG = 3e38
SCALE = math.log2(math.e) / math.sqrt(HS)


def place(x, y, z, core):
    return (y * 8 + z % 8, 4 * x + 2 * (z // 8) + core)


def main_kernel(
    q_ref, k_ref, v_ref, w_hbm, slen_ref, wstart_ref, out_ref,
    w_ref, w_sem, pack, ex_s, ex_r, stage, send_q, send_kv, kv, vt, qbuf, qt, acc, stat, pos_ref, row_ref, wf,
    robuf, rstat, obuf, send_o, att, fs, send_c, recv_c, send_x, recv_x,
    ex_ss, ex_rs, zq_s, zq_r, zk_s, zk_r, xk_s, xk_r, q_s, q_r, wz_s, wz_r, wy_s, wy_r,
    o_s, o_r, st_s, st_r, a_s, a_r, c_s, c_r, x_s, x_r,
):
    span = lax.axis_index("span")
    head = lax.axis_index("head")
    y, zlo = span // 8, span % 8
    x, zhi, core = head // 4, (head // 2) % 2, head % 2
    z = zhi * 8 + zlo
    quad = z // 4

    def copy(src, dst, ssem, rsem, dev):
        return pltpu.make_async_remote_copy(
            src_ref=src, dst_ref=dst, send_sem=ssem, recv_sem=rsem, device_id=dev, device_id_type=MESH
        )

    def zdev(d):
        return place(x, y, (z + d) % NZ, core)

    def ydev(d):
        return place(x, (y + d) % 4, z, core)

    def xdev(d):
        return place((x + d) % 4, y, z, core)

    twin = place(x, y, z, 1 - core)

    barrier = pltpu.get_barrier_semaphore()

    def greet(dev):
        pl.semaphore_signal(barrier, inc=1, device_id=dev, device_id_type=MESH)

    greet(twin)
    for d in range(1, 4):
        greet(ydev(d))
        greet(xdev(d))

    def greet_z(d, carry):
        greet(zdev(d))
        return carry

    lax.fori_loop(1, NZ, greet_z, 0)

    def greet_o(n, carry):
        sx, sz = n // 4, 4 * x + n % 4

        @pl.when((sx != x) | (sz != z))
        def _():
            greet(place(sx, y, sz, core))

        return carry

    lax.fori_loop(0, NZ, greet_o, 0)

    def pack_tensor(ref, slot):
        def one(n, carry):
            col = 128 * (8 * (n // 4) + 4 * ((n // 2) % 2) + n % 2)
            row = pl.ds(pl.multiple_of(n * ROWS, 8), ROWS)
            theirs = ref[:, pl.ds(pl.multiple_of(col + 256 * (1 - core), 128), 128)]
            pack[row, :] = theirs.astype(F32)
            mine = ref[:, pl.ds(pl.multiple_of(col + 256 * core, 128), 128)]
            stage[slot, pl.ds(pl.multiple_of(n * 48 + core * ROWS, 8), ROWS), :] = mine.astype(F32)
            return carry

        lax.fori_loop(0, NZ, one, 0)
        ex_s[slot] = pack[...].astype(BF16)

    def ex_copy(slot):
        return copy(ex_s.at[slot], ex_r.at[slot], ex_ss.at[slot], ex_rs.at[slot], twin)

    def unpack_tensor(slot):
        ex_copy(slot).wait_recv()
        pack[...] = ex_r[slot].astype(F32)

        def one(n, carry):
            stage[slot, pl.ds(pl.multiple_of(n * 48 + (1 - core) * ROWS, 8), ROWS), :] = pack[
                pl.ds(pl.multiple_of(n * ROWS, 8), ROWS), :
            ]
            return carry

        lax.fori_loop(0, NZ, one, 0)
        return stage[slot].astype(BF16)

    side = (zdev(1), zdev(NZ - 1))

    def wz_forward(direction, i):
        c = 2 * y + direction
        rows = pl.ds(pl.multiple_of(i * PIECE, PIECE), PIECE)
        return copy(
            wf.at[c, rows], wf.at[c, rows], wz_s.at[direction, i], wz_r.at[direction, i], side[direction]
        )

    def wz_origin(direction, i):
        c = 2 * y + direction
        rows = pl.ds(pl.multiple_of(i * PIECE, PIECE), PIECE)
        cols = pl.ds(pl.multiple_of(c * CHUNK, 128), CHUNK)
        return copy(
            w_hbm.at[rows, cols], wf.at[c, rows], wz_s.at[direction, i], wz_r.at[direction, i], side[direction]
        )

    def wy_copy(direction, i, d):
        c = 2 * y + direction
        rows = pl.ds(pl.multiple_of(i * PIECE, PIECE), PIECE)
        return copy(
            wf.at[c, rows], wf.at[c, rows], wy_s.at[direction, i, d - 1], wy_r.at[direction, i, d - 1], ydev(d)
        )

    def weight_start():
        for direction in range(2):

            @pl.when(zlo == (7 if direction == 0 else 0))
            def _(direction=direction):
                def go(i, carry):
                    wz_origin(direction, i).start()
                    return carry

                lax.fori_loop(0, NP, go, 0)

    def weight_point(u):
        for direction in range(2):
            hop = zlo if direction == 0 else 7 - zlo
            i = u - hop

            @pl.when((i >= 0) & (i < NP))
            def _(direction=direction, hop=hop, i=i):
                wz_forward(direction, i).wait_recv()

                @pl.when(hop < 7)
                def _():
                    wz_forward(direction, i).start()

                for d in range(1, 4):
                    wy_copy(direction, i, d).start()

    own_weight = pltpu.make_async_copy(w_hbm, w_ref, w_sem)
    own_weight.start()
    pack_tensor(q_ref, 0)
    pl.semaphore_wait(barrier, 1 + 3 + 3 + 15 + 16 - jnp.where(quad == x, 1, 0))
    ex_copy(0).start()
    weight_start()
    pack_tensor(k_ref, 1)
    ex_copy(1).start()
    pack_tensor(v_ref, 2)
    ex_copy(2).start()

    def zrows(n):
        return pl.ds(pl.multiple_of(n * 48, 16), 48)

    def zq_copy(d):
        to = (z + d) % NZ
        return copy(send_q.at[zrows(to)], qbuf.at[y, zrows(z)], zq_s.at[d - 1], zq_r.at[d - 1], zdev(d))

    def zq_in(d):
        src = (z + NZ - d) % NZ
        return copy(send_q.at[zrows(src)], qbuf.at[y, zrows(src)], zq_s.at[d - 1], zq_r.at[d - 1], zdev(d))

    def zk_copy(d):
        to = (z + d) % NZ
        return copy(
            send_kv.at[:, zrows(to)], kv.at[:, z, zrows(x)], zk_s.at[d - 1], zk_r.at[d - 1], zdev(d)
        )

    def zk_in(d):
        src = (z + NZ - d) % NZ
        return copy(
            send_kv.at[:, zrows(src)], kv.at[:, src, zrows(x)], zk_s.at[d - 1], zk_r.at[d - 1], zdev(d)
        )

    def start_both_ways(what):
        def one(t, carry):
            what(t).start()
            what(NZ - t).start()
            return carry

        lax.fori_loop(1, 8, one, 0)
        what(8).start()

    send_q[...] = unpack_tensor(0)
    start_both_ways(zq_copy)
    qbuf[y, zrows(z), :] = send_q[zrows(z), :]
    send_kv[0] = unpack_tensor(1)
    send_kv[1] = unpack_tensor(2)
    start_both_ways(zk_copy)
    weight_point(0)
    for tensor in range(2):
        kv[tensor, z, zrows(x), :] = send_kv[tensor, zrows(z), :]

    def xk_copy(n, d):
        part = kv.at[:, n, zrows(x)]
        return copy(part, part, xk_s.at[n, d - 1], xk_r.at[n, d - 1], xdev(d))

    def xk_in(n, d):
        part = kv.at[:, n, zrows((x + 4 - d) % 4)]
        return copy(part, part, xk_s.at[n, d - 1], xk_r.at[n, d - 1], xdev(d))

    def spread(n):
        for d in (2, 1, 3):
            xk_copy(n, d).start()

    def spread_pair(t):
        zk_in(t).wait_recv()
        spread((z + NZ - t) % NZ)

        @pl.when(t < 8)
        def _():
            zk_in(NZ - t).wait_recv()
            spread((z + t) % NZ)

    def gathered(n):
        for d in range(1, 4):
            xk_in(n, d).wait_recv()

    spread(z)

    r = lax.broadcasted_iota(jnp.int32, (HALF, 128), 0)
    rx = jnp.where(r >= 48, 1, 0) + jnp.where(r >= 96, 1, 0) + jnp.where(r >= 144, 1, 0)
    pos_ref[...] = r + 48 * rx
    lane = lax.broadcasted_iota(jnp.int32, (8, NQ), 1)
    lz = jnp.zeros((8, NQ), jnp.int32)
    for n in range(1, NZ):
        lz = lz + jnp.where(lane >= 48 * n, 1, 0)
    lz = lz - jnp.where(lz >= 8, 8, 0)
    row_ref[4] = lz

    def first_rows(yy, carry):
        first = jnp.full((8, NQ), wstart_ref[8 * yy], jnp.int32)
        for n in range(1, 8):
            first = jnp.where(lz == n, wstart_ref[8 * yy + n], first)
        row_ref[yy] = first
        stat[yy] = jnp.where(lax.broadcasted_iota(jnp.int32, (8, NQ), 0) < 1, NEG, 0.0).astype(F32)
        acc[yy] = jnp.zeros((ACC, NQ), F32)
        return carry

    lax.fori_loop(0, 4, first_rows, 0)

    def zq_wait(d, carry):
        zq_in(d).wait_recv()
        return carry

    lax.fori_loop(1, NZ, zq_wait, 0)

    def q_copy(d):
        return copy(qbuf.at[y], qbuf.at[y], q_s.at[d - 1], q_r.at[d - 1], ydev(4 - d))

    def q_in(d):
        src = (y + d) % 4
        return copy(qbuf.at[src], qbuf.at[src], q_s.at[d - 1], q_r.at[d - 1], ydev(d))

    for d in range(1, 4):

        @pl.when(y - d >= 0)
        def _(d=d):
            q_copy(d).start()

    weight_point(1)
    spread_pair(1)
    spread_pair(2)
    weight_point(2)
    spread_pair(3)

    def turn(yy):
        qt[yy] = qbuf[yy].astype(F32).T.astype(BF16)

    turn(y)

    def blocks(t):
        return (z + NZ - t) % NZ, jnp.where(t == 8, z, (z + t) % NZ)

    def attend(t, low, high):
        sides = []
        for n in blocks(t):
            j = 8 * y + n % 8
            cap = jnp.where(pos_ref[...] + 48 * (n // 8) < slen_ref[j], BIG, NEG).astype(F32)
            sides.append((j, jnp.concatenate([cap, cap], axis=1)))
        za, zb = blocks(t)
        k2 = jnp.concatenate([kv[0, za], kv[0, zb]], axis=0)
        v2 = vt[t - 1]

        def one_row(yy, carry):
            rows = [(row_ref[yy] <= j) & (j <= 8 * yy + row_ref[4]) for j, cap in sides]
            olds = stat[yy, pl.ds(0, 1), :]
            tiles = [slice(n * TILE, (n + 1) * TILE) for n in range(NQ // TILE)]
            scores = [jnp.dot(k2, qt[yy, :, cols], preferred_element_type=F32) for cols in tiles]
            tops, sums = [], []
            for cols, s in zip(tiles, scores):
                top = olds[:, cols]
                parts = []
                for n in range(2):
                    part = jnp.minimum(s[n * HALF : (n + 1) * HALF] * SCALE, sides[n][1])
                    vis = rows[n][0:1, cols]
                    top = jnp.maximum(top, jnp.where(vis, jnp.max(part, axis=0, keepdims=True), NEG))
                    parts.append((part, vis))
                weight = jnp.concatenate(
                    [jnp.exp2(part - jnp.where(vis, top, BIG)).astype(BF16) for part, vis in parts], axis=0
                )
                tops.append(top)
                sums.append(jnp.dot(v2, weight, preferred_element_type=F32))
            for cols, top, part in zip(tiles, tops, sums):
                factor = jnp.exp2(olds[:, cols] - top)
                acc[yy, :, cols] = acc[yy, :, cols] * factor + part[:ACC]
                stat[yy, pl.ds(0, 1), cols] = top
            return carry

        lax.fori_loop(low, high, one_row, 0)

    def finished(yy):
        total = acc[yy, pl.ds(HS, 1), :]
        stat[yy, pl.ds(1, 1), :] = total
        return (acc[yy, pl.ds(0, HS), :] * (1.0 / jnp.maximum(total, 1e-30))).astype(BF16)

    def o_copy(yy, d):
        return (
            copy(stat.at[yy], rstat.at[y], st_s.at[d - 1], st_r.at[d - 1], place(x, yy, z, core)),
            copy(obuf.at[yy], robuf.at[y], o_s.at[d - 1], o_r.at[d - 1], place(x, yy, z, core)),
        )

    def o_in(d):
        src = (y + 4 - d) % 4
        return (
            copy(stat.at[src], rstat.at[src], st_s.at[d - 1], st_r.at[d - 1], ydev(4 - d)),
            copy(obuf.at[src], robuf.at[src], o_s.at[d - 1], o_r.at[d - 1], ydev(4 - d)),
        )

    def give(yy):
        @pl.when(yy == y)
        def _():
            robuf[yy] = finished(yy)
            rstat[yy] = stat[yy]

        for d in range(1, 4):

            @pl.when(y + d == yy)
            def _(d=d):
                obuf[yy] = finished(yy)
                for one in o_copy(yy, d):
                    one.start()

    def arrive(t):
        @pl.when(t < 6)
        def _():
            spread_pair(t + 3)

        for n in blocks(t):
            gathered(n)
        za, zb = blocks(t)
        vt[t - 1, pl.ds(0, HS), :] = jnp.concatenate([kv[1, za], kv[1, zb]], axis=0).T
        vt[t - 1, pl.ds(HS, VT - HS), :] = jnp.ones((VT - HS, 2 * HALF), BF16)

    def own_step(t, carry):
        arrive(t)
        attend(t, y, y + 1)
        weight_point(t + 2)
        return carry

    def full_step(t, carry):
        arrive(t)
        attend(t, y, 4)
        weight_point(t + 2)
        return carry

    lax.fori_loop(1, EARLY + 1, own_step, 0)
    for d in range(1, 4):

        @pl.when(y + d <= 3)
        def _(d=d):
            q_in(d).wait_recv()
            turn(y + d)

    lax.fori_loop(EARLY + 1, 9, full_step, 0)

    for yy in (3, 2, 1):

        @pl.when(y < yy)
        def _(yy=yy):
            def one(t, carry):
                attend(t, yy, yy + 1)
                return carry

            lax.fori_loop(1, EARLY + 1, one, 0)

        give(yy)
    give(0)
    for d in range(1, 4):

        @pl.when(y + d <= 3)
        def _(d=d):
            rstat[y + d] = jnp.where(lax.broadcasted_iota(jnp.int32, (8, NQ), 0) < 1, NEG, 0.0).astype(F32)
            robuf[y + d] = jnp.zeros((HS, NQ), BF16)

        @pl.when(y - d >= 0)
        def _(d=d):
            for one in o_in(d):
                one.wait_recv()

    tops = [rstat[yy, pl.ds(0, 1), :] for yy in range(4)]
    best = jnp.maximum(jnp.maximum(tops[0], tops[1]), jnp.maximum(tops[2], tops[3]))
    shares = [rstat[yy, pl.ds(1, 1), :] * jnp.exp2(tops[yy] - best) for yy in range(4)]
    inv = 1.0 / (shares[0] + shares[1] + shares[2] + shares[3])
    mixed = jnp.zeros((HS, NQ), F32)
    for yy in range(4):
        mixed = mixed + robuf[yy].astype(F32) * (shares[yy] * inv)
    send_o[...] = mixed.T.astype(BF16)

    def a_copy(n):
        return copy(
            send_o.at[zrows(n)], att.at[z % 4, zrows(x)], a_s.at[n], a_r.at[x * 4 + z % 4], place(quad, y, n, core)
        )

    def a_in(n):
        sx = n // 4
        return copy(
            send_o.at[zrows(n)], att.at[n % 4, zrows(sx)], a_s.at[n], a_r.at[n], place(sx, y, 4 * x + n % 4, core)
        )

    def a_send(n, carry):
        to = (z + n) % NZ

        @pl.when((to != z) | (quad != x))
        def _():
            a_copy(to).start()

        return carry

    lax.fori_loop(0, NZ, a_send, 0)

    @pl.when(quad == x)
    def _():
        att[z % 4, zrows(x), :] = send_o[zrows(z), :]

    for slot in range(3):
        ex_copy(slot).wait_send()

    def z_end(d, carry):
        zq_copy(d).wait_send()
        zk_copy(d).wait_send()
        return carry

    lax.fori_loop(1, NZ, z_end, 0)

    def n_end(n, carry):
        for d in range(1, 4):
            xk_copy(n, d).wait_send()

        return carry

    lax.fori_loop(0, NZ, n_end, 0)

    def w_end(i, carry):
        for direction in range(2):
            wz_forward(direction, i).wait_send()
            for d in range(1, 4):
                wy_copy(direction, i, d).wait_send()
        return carry

    lax.fori_loop(0, NP, w_end, 0)
    for d in range(1, 4):

        @pl.when(y - d >= 0)
        def _(d=d):
            q_copy(d).wait_send()

        @pl.when(y + d <= 3)
        def _(d=d):
            for one in o_copy(y + d, d):
                one.wait_send()

    own_weight.wait()

    def wy_wait(n, carry):
        direction, i = n // NP, n % NP
        rows = pl.ds(pl.multiple_of(i * PIECE, PIECE), PIECE)
        for d in range(1, 4):
            c = 2 * ((y + 4 - d) % 4) + direction
            copy(
                wf.at[c, rows], wf.at[c, rows], wy_s.at[direction, i, d - 1], wy_r.at[direction, i, d - 1], ydev(d)
            ).wait_recv()
        return carry

    lax.fori_loop(0, 2 * NP, wy_wait, 0)

    def a_wait(n, carry):
        @pl.when((n // 4 != x) | (4 * x + n % 4 != z))
        def _():
            a_in(n).wait_recv()

        return carry

    lax.fori_loop(0, NZ, a_wait, 0)

    def c_copy(n):
        return copy(send_c.at[n], recv_c.at[n], c_s.at[n], c_r.at[n], twin)

    def core_rows(n, c):
        return jnp.concatenate(
            [fs[n, pl.ds(pl.multiple_of(xx * 48 + c * ROWS, 8), ROWS), :] for xx in range(4)], axis=0
        )

    def project(n):
        cols = pl.ds(pl.multiple_of(n * CHUNK, 128), CHUNK)
        near = jnp.concatenate([att[2 * zhi], att[2 * zhi + 1]], axis=1)
        far = jnp.concatenate([att[2 - 2 * zhi], att[3 - 2 * zhi]], axis=1)
        fs[n] = jnp.dot(near, w_ref[:, cols], preferred_element_type=F32) + jnp.dot(
            far, wf[n], preferred_element_type=F32
        )
        send_c[n] = core_rows(n, 1 - core).astype(BF16)
        c_copy(n).start()

    def x_copy(g, d):
        to = (x + d) % 4
        return copy(
            send_x.at[g, to], recv_x.at[g, x], x_s.at[g, d - 1], x_r.at[g, d - 1], xdev(d)
        )

    def x_in(g, d):
        src = (x + 4 - d) % 4
        return copy(
            send_x.at[g, src], recv_x.at[g, src], x_s.at[g, d - 1], x_r.at[g, d - 1], xdev(d)
        )

    def pair_sum(g):
        parts = []
        for n in range(2):
            c_copy(2 * g + n).wait_recv()
            parts.append(core_rows(2 * g + n, core) + recv_c[2 * g + n].astype(F32))
        for xx in range(4):
            send_x[g, xx] = jnp.concatenate([part[xx * ROWS : (xx + 1) * ROWS] for part in parts], axis=0).astype(BF16)
        for d in (2, 1, 3):
            x_copy(g, d).start()

    def output_step(g, carry):
        @pl.when(g < 4)
        def _():
            project(2 * g)
            project(2 * g + 1)

        @pl.when(g > 0)
        def _():
            pair_sum(g - 1)

        return carry

    lax.fori_loop(0, 5, output_step, 0)

    def collect(g, carry):
        total = send_x[g, x].astype(F32)
        for d in range(1, 4):
            x_in(g, d).wait_recv()
            total = total + recv_x[g, (x + 4 - d) % 4].astype(F32)
        for n in range(2):
            out_ref[:, pl.ds(pl.multiple_of((2 * g + n) * CHUNK, 128), CHUNK)] = total[n * ROWS : (n + 1) * ROWS]
        return carry

    lax.fori_loop(0, 4, collect, 0)

    def c_end(n, carry):
        c_copy(n).wait_send()
        return carry

    lax.fori_loop(0, 8, c_end, 0)

    def a_end(n, carry):
        @pl.when((n != z) | (quad != x))
        def _():
            a_copy(n).wait_send()

        return carry

    lax.fori_loop(0, NZ, a_end, 0)

    def x_end(g, carry):
        for d in range(1, 4):
            x_copy(g, d).wait_send()
        return carry

    lax.fori_loop(0, 4, x_end, 0)


def last_kernel(proj_ref, gate_ref, lat_ref, step_ref, len_ref, vel_ref, adv_ref):
    span = lax.axis_index("span")
    head = lax.axis_index("head")
    level = step_ref[span]
    length = len_ref[span]

    def sigma_of(step):
        fraction = 1.0 - step / STEPS
        return 8.0 * fraction / (1.0 + 7.0 * fraction)

    now = jnp.full((ROWS, 128), level, jnp.int32).astype(F32)
    dt = sigma_of(now + 1.0) - sigma_of(now)
    spot = head * ROWS + lax.broadcasted_iota(jnp.int32, (ROWS, 128), 0)
    live = jnp.where(spot < length, 1.0, 0.0).astype(F32)
    wide = 512
    dt_w = jnp.concatenate([dt] * (wide // 128), axis=1)
    live_w = jnp.concatenate([live] * (wide // 128), axis=1)
    for n in range(D // wide):
        cols = pl.ds(n * wide, wide)
        gate = gate_ref[pl.ds(level, 1), cols]
        vel = (gate * proj_ref[:, cols] * live_w).astype(BF16)
        vel_ref[:, cols] = vel
        adv_ref[:, cols] = lat_ref[:, cols] + dt_w * vel.astype(F32)


def body(query, keys, values, out_weight, time_gates, noise_step, span_length, window_start, latent):
    vmem = pl.BlockSpec(memory_space=pltpu.VMEM)
    smem = pl.BlockSpec(memory_space=pltpu.SMEM)
    dma = pltpu.SemaphoreType.DMA
    projected = pl.pallas_call(
        main_kernel,
        out_shape=jax.ShapeDtypeStruct((ROWS, D), F32),
        in_specs=[vmem, vmem, vmem, pl.BlockSpec(memory_space=pl.ANY), smem, smem],
        out_specs=vmem,
        scratch_shapes=[
            pltpu.VMEM((256, D), BF16),
            dma,
            pltpu.VMEM((NZ * ROWS, 128), F32),
            pltpu.VMEM((3, NZ * ROWS, 128), BF16),
            pltpu.VMEM((3, NZ * ROWS, 128), BF16),
            pltpu.VMEM((3, NQ, 128), F32),
            pltpu.VMEM((NQ, 128), BF16),
            pltpu.VMEM((2, NQ, 128), BF16),
            pltpu.VMEM((2, NZ, HALF, 128), BF16),
            pltpu.VMEM((8, VT, 2 * HALF), BF16),
            pltpu.VMEM((4, NQ, 128), BF16),
            pltpu.VMEM((4, HS, NQ), BF16),
            pltpu.VMEM((4, ACC, NQ), F32),
            pltpu.VMEM((4, 8, NQ), F32),
            pltpu.VMEM((HALF, 128), jnp.int32),
            pltpu.VMEM((5, 8, NQ), jnp.int32),
            pltpu.VMEM((8, 256, CHUNK), BF16),
            pltpu.VMEM((4, HS, NQ), BF16),
            pltpu.VMEM((4, 8, NQ), F32),
            pltpu.VMEM((4, HS, NQ), BF16),
            pltpu.VMEM((NQ, 128), BF16),
            pltpu.VMEM((4, HALF, 128), BF16),
            pltpu.VMEM((8, HALF, CHUNK), F32),
            pltpu.VMEM((8, 96, CHUNK), BF16),
            pltpu.VMEM((8, 96, CHUNK), BF16),
            pltpu.VMEM((4, 4, 48, CHUNK), BF16),
            pltpu.VMEM((4, 4, 48, CHUNK), BF16),
            dma((3,)), dma((3,)),
            dma((15,)), dma((15,)),
            dma((15,)), dma((15,)),
            dma((NZ, 3)), dma((NZ, 3)),
            dma((3,)), dma((3,)),
            dma((2, NP)), dma((2, NP)),
            dma((2, NP, 3)), dma((2, NP, 3)),
            dma((3,)), dma((3,)),
            dma((3,)), dma((3,)),
            dma((NZ,)), dma((NZ,)),
            dma((8,)), dma((8,)),
            dma((4, 3)), dma((4, 3)),
        ],
        compiler_params=pltpu.CompilerParams(
            collective_id=0, has_side_effects=True, vmem_limit_bytes=40 * 1024 * 1024
        ),
        name="attention_tick",
    )(query, keys, values, out_weight, span_length, window_start)
    return pl.pallas_call(
        last_kernel,
        out_shape=(jax.ShapeDtypeStruct((ROWS, D), BF16), jax.ShapeDtypeStruct((ROWS, D), F32)),
        in_specs=[vmem, vmem, vmem, smem, smem],
        out_specs=(vmem, vmem),
        compiler_params=pltpu.CompilerParams(vmem_limit_bytes=32 * 1024 * 1024),
        name="euler_update",
    )(projected, time_gates, latent, noise_step, span_length)


def solution(mesh):
    rows = P(("span", "head"), None)
    return jax.shard_map(
        body,
        mesh=mesh,
        in_specs=(rows, rows, rows, P("head", None), P(), P(), P(), P(), rows),
        out_specs=(rows, rows),
        check_vma=False,
    )
```

```python
import functools
import math

import jax
import jax.numpy as jnp
from jax import lax
from jax.experimental import pallas as pl
from jax.experimental.pallas import tpu as pltpu
from jax.sharding import PartitionSpec as P

MESH = pl.DeviceIdType.MESH
F32 = jnp.float32
BF16 = jnp.bfloat16

D = 5120
HS = 128
STEPS = 30
ROWS = 24
HALF = 192
NQ = 768
NZ = 16
CHUNK = 640
PIECE = 64
NP = 4
EARLY = 2
TILE = 256
VT = HS + 16
ACC = HS + 8
NEG = -1e30
BIG = 3e38
SCALE = math.log2(math.e) / math.sqrt(HS)


def place(x, y, z, core):
    return (y * 8 + z % 8, 4 * x + 2 * (z // 8) + core)


def main_kernel(
    q_ref, k_ref, v_ref, w_hbm, slen_ref, wstart_ref, out_ref,
    w_ref, w_sem, pack, ex_s, ex_r, stage, send_q, send_kv, kv, vt, qbuf, qt, acc, stat, pos_ref, row_ref, wf,
    robuf, rstat, obuf, send_o, att, fs, send_c, recv_c, send_x, recv_x,
    ex_ss, ex_rs, zq_s, zq_r, zk_s, zk_r, xk_s, xk_r, q_s, q_r, wz_s, wz_r, wy_s, wy_r,
    o_s, o_r, st_s, st_r, a_s, a_r, c_s, c_r, x_s, x_r,
):
    span = lax.axis_index("span")
    head = lax.axis_index("head")
    y, zlo = span // 8, span % 8
    x, zhi, core = head // 4, (head // 2) % 2, head % 2
    z = zhi * 8 + zlo
    quad = (z // 4 + 2 * core) % 4
    fours = (x + 2 * core) % 4

    def copy(src, dst, ssem, rsem, dev):
        return pltpu.make_async_remote_copy(
            src_ref=src, dst_ref=dst, send_sem=ssem, recv_sem=rsem, device_id=dev, device_id_type=MESH
        )

    def zdev(d):
        return place(x, y, (z + d) % NZ, core)

    def ydev(d):
        return place(x, (y + d) % 4, z, core)

    def xdev(d):
        return place((x + d) % 4, y, z, core)

    twin = place(x, y, z, 1 - core)

    barrier = pltpu.get_barrier_semaphore()

    def greet(dev):
        pl.semaphore_signal(barrier, inc=1, device_id=dev, device_id_type=MESH)

    greet(twin)
    for d in range(1, 4):
        greet(ydev(d))
        greet(xdev(d))

    def greet_z(d, carry):
        greet(zdev(d))
        return carry

    lax.fori_loop(1, NZ, greet_z, 0)

    def greet_o(n, carry):
        sx, sz = n // 4, 4 * fours + n % 4

        @pl.when((sx != x) | (sz != z))
        def _():
            greet(place(sx, y, sz, core))

        return carry

    lax.fori_loop(0, NZ, greet_o, 0)

    def pack_tensor(ref, slot):
        def one(n, carry):
            low = 128 * (4 * ((n // 2) % 2) + n % 2)
            col = low + 1024 * ((n // 4 + 2 * core) % 4) + 256 * core
            other = low + 1024 * ((n // 4 + 2 * (1 - core)) % 4) + 256 * (1 - core)
            row = pl.ds(pl.multiple_of(n * ROWS, 8), ROWS)
            theirs = ref[:, pl.ds(pl.multiple_of(other, 128), 128)]
            pack[row, :] = theirs.astype(F32)
            mine = ref[:, pl.ds(pl.multiple_of(col, 128), 128)]
            stage[slot, pl.ds(pl.multiple_of(n * 48 + core * ROWS, 8), ROWS), :] = mine.astype(F32)
            return carry

        lax.fori_loop(0, NZ, one, 0)
        ex_s[slot] = pack[...].astype(BF16)

    def ex_copy(slot):
        return copy(ex_s.at[slot], ex_r.at[slot], ex_ss.at[slot], ex_rs.at[slot], twin)

    def unpack_tensor(slot):
        ex_copy(slot).wait_recv()
        pack[...] = ex_r[slot].astype(F32)

        def one(n, carry):
            stage[slot, pl.ds(pl.multiple_of(n * 48 + (1 - core) * ROWS, 8), ROWS), :] = pack[
                pl.ds(pl.multiple_of(n * ROWS, 8), ROWS), :
            ]
            return carry

        lax.fori_loop(0, NZ, one, 0)
        return stage[slot].astype(BF16)

    side = (zdev(1), zdev(NZ - 1))

    def wz_forward(direction, i):
        c = 2 * y + direction
        rows = pl.ds(pl.multiple_of(i * PIECE, PIECE), PIECE)
        return copy(
            wf.at[c, rows], wf.at[c, rows], wz_s.at[direction, i], wz_r.at[direction, i], side[direction]
        )

    def wz_origin(direction, i):
        c = 2 * y + direction
        rows = pl.ds(pl.multiple_of(i * PIECE, PIECE), PIECE)
        cols = pl.ds(pl.multiple_of(c * CHUNK, 128), CHUNK)
        return copy(
            w_hbm.at[rows, cols], wf.at[c, rows], wz_s.at[direction, i], wz_r.at[direction, i], side[direction]
        )

    def wy_copy(direction, i, d):
        c = 2 * y + direction
        rows = pl.ds(pl.multiple_of(i * PIECE, PIECE), PIECE)
        return copy(
            wf.at[c, rows], wf.at[c, rows], wy_s.at[direction, i, d - 1], wy_r.at[direction, i, d - 1], ydev(d)
        )

    def weight_start():
        for direction in range(2):

            @pl.when(zlo == (7 if direction == 0 else 0))
            def _(direction=direction):
                def go(i, carry):
                    wz_origin(direction, i).start()
                    return carry

                lax.fori_loop(0, NP, go, 0)

    def weight_point(u):
        for direction in range(2):
            hop = zlo if direction == 0 else 7 - zlo
            i = u - hop

            @pl.when((i >= 0) & (i < NP))
            def _(direction=direction, hop=hop, i=i):
                wz_forward(direction, i).wait_recv()

                @pl.when(hop < 7)
                def _():
                    wz_forward(direction, i).start()

                for d in range(1, 4):
                    wy_copy(direction, i, d).start()

    own_weight = pltpu.make_async_copy(w_hbm, w_ref, w_sem)
    own_weight.start()
    pack_tensor(q_ref, 0)
    pl.semaphore_wait(barrier, 1 + 3 + 3 + 15 + 16 - jnp.where(quad == x, 1, 0))
    ex_copy(0).start()
    weight_start()
    pack_tensor(k_ref, 1)
    ex_copy(1).start()
    pack_tensor(v_ref, 2)
    ex_copy(2).start()

    def zrows(n):
        return pl.ds(pl.multiple_of(n * 48, 16), 48)

    def zq_copy(d):
        to = (z + d) % NZ
        return copy(send_q.at[zrows(to)], qbuf.at[y, zrows(z)], zq_s.at[d - 1], zq_r.at[d - 1], zdev(d))

    def zq_in(d):
        src = (z + NZ - d) % NZ
        return copy(send_q.at[zrows(src)], qbuf.at[y, zrows(src)], zq_s.at[d - 1], zq_r.at[d - 1], zdev(d))

    def zk_copy(d):
        to = (z + d) % NZ
        return copy(
            send_kv.at[:, zrows(to)], kv.at[:, z, zrows(x)], zk_s.at[d - 1], zk_r.at[d - 1], zdev(d)
        )

    def zk_in(d):
        src = (z + NZ - d) % NZ
        return copy(
            send_kv.at[:, zrows(src)], kv.at[:, src, zrows(x)], zk_s.at[d - 1], zk_r.at[d - 1], zdev(d)
        )

    def start_both_ways(what):
        def one(t, carry):
            what(t).start()
            what(NZ - t).start()
            return carry

        lax.fori_loop(1, 8, one, 0)
        what(8).start()

    send_q[...] = unpack_tensor(0)
    start_both_ways(zq_copy)
    qbuf[y, zrows(z), :] = send_q[zrows(z), :]
    send_kv[0] = unpack_tensor(1)
    send_kv[1] = unpack_tensor(2)
    start_both_ways(zk_copy)
    weight_point(0)
    for tensor in range(2):
        kv[tensor, z, zrows(x), :] = send_kv[tensor, zrows(z), :]

    def xk_copy(n, d):
        part = kv.at[:, n, zrows(x)]
        return copy(part, part, xk_s.at[n, d - 1], xk_r.at[n, d - 1], xdev(d))

    def xk_in(n, d):
        part = kv.at[:, n, zrows((x + 4 - d) % 4)]
        return copy(part, part, xk_s.at[n, d - 1], xk_r.at[n, d - 1], xdev(d))

    def spread(n):
        for d in (2, 1, 3):
            xk_copy(n, d).start()

    def spread_pair(t):
        zk_in(t).wait_recv()
        spread((z + NZ - t) % NZ)

        @pl.when(t < 8)
        def _():
            zk_in(NZ - t).wait_recv()
            spread((z + t) % NZ)

    def gathered(n):
        for d in range(1, 4):
            xk_in(n, d).wait_recv()

    spread(z)

    r = lax.broadcasted_iota(jnp.int32, (HALF, 128), 0)
    rx = jnp.where(r >= 48, 1, 0) + jnp.where(r >= 96, 1, 0) + jnp.where(r >= 144, 1, 0)
    pos_ref[...] = r + 48 * rx
    lane = lax.broadcasted_iota(jnp.int32, (8, NQ), 1)
    lz = jnp.zeros((8, NQ), jnp.int32)
    for n in range(1, NZ):
        lz = lz + jnp.where(lane >= 48 * n, 1, 0)
    lz = lz - jnp.where(lz >= 8, 8, 0)
    row_ref[4] = lz

    def first_rows(yy, carry):
        first = jnp.full((8, NQ), wstart_ref[8 * yy], jnp.int32)
        for n in range(1, 8):
            first = jnp.where(lz == n, wstart_ref[8 * yy + n], first)
        row_ref[yy] = first
        stat[yy] = jnp.where(lax.broadcasted_iota(jnp.int32, (8, NQ), 0) < 1, NEG, 0.0).astype(F32)
        acc[yy] = jnp.zeros((ACC, NQ), F32)
        return carry

    lax.fori_loop(0, 4, first_rows, 0)

    def zq_wait(d, carry):
        zq_in(d).wait_recv()
        return carry

    lax.fori_loop(1, NZ, zq_wait, 0)

    def q_copy(d):
        return copy(qbuf.at[y], qbuf.at[y], q_s.at[d - 1], q_r.at[d - 1], ydev(4 - d))

    def q_in(d):
        src = (y + d) % 4
        return copy(qbuf.at[src], qbuf.at[src], q_s.at[d - 1], q_r.at[d - 1], ydev(d))

    for d in range(1, 4):

        @pl.when(y - d >= 0)
        def _(d=d):
            q_copy(d).start()

    weight_point(1)
    spread_pair(1)
    spread_pair(2)
    weight_point(2)
    spread_pair(3)
    spread_pair(4)

    def turn(yy):
        qt[yy] = qbuf[yy].astype(F32).T.astype(BF16)

    turn(y)

    def blocks(t):
        return (z + NZ - t) % NZ, jnp.where(t == 8, z, (z + t) % NZ)

    def attend(t, low, high):
        sides = []
        for n in blocks(t):
            j = 8 * y + n % 8
            cap = jnp.where(pos_ref[...] + 48 * (n // 8) < slen_ref[j], BIG, NEG).astype(F32)
            sides.append((j, jnp.concatenate([cap, cap], axis=1)))
        za, zb = blocks(t)
        k2 = jnp.concatenate([kv[0, za], kv[0, zb]], axis=0)
        v2 = vt[t - 1]

        def one_row(yy, carry):
            rows = [(row_ref[yy] <= j) & (j <= 8 * yy + row_ref[4]) for j, cap in sides]
            olds = stat[yy, pl.ds(0, 1), :]
            tiles = [slice(n * TILE, (n + 1) * TILE) for n in range(NQ // TILE)]
            scores = [jnp.dot(k2, qt[yy, :, cols], preferred_element_type=F32) for cols in tiles]
            tops, sums = [], []
            for cols, s in zip(tiles, scores):
                top = olds[:, cols]
                parts = []
                for n in range(2):
                    part = jnp.minimum(s[n * HALF : (n + 1) * HALF] * SCALE, sides[n][1])
                    vis = rows[n][0:1, cols]
                    top = jnp.maximum(top, jnp.where(vis, jnp.max(part, axis=0, keepdims=True), NEG))
                    parts.append((part, vis))
                weight = jnp.concatenate(
                    [jnp.exp2(part - jnp.where(vis, top, BIG)).astype(BF16) for part, vis in parts], axis=0
                )
                tops.append(top)
                sums.append(jnp.dot(v2, weight, preferred_element_type=F32))
            for cols, top, part in zip(tiles, tops, sums):
                factor = jnp.exp2(olds[:, cols] - top)
                acc[yy, :, cols] = acc[yy, :, cols] * factor + part[:ACC]
                stat[yy, pl.ds(0, 1), cols] = top
            return carry

        lax.fori_loop(low, high, one_row, 0)

    def finished(yy):
        total = acc[yy, pl.ds(HS, 1), :]
        stat[yy, pl.ds(1, 1), :] = total
        return (acc[yy, pl.ds(0, HS), :] * (1.0 / jnp.maximum(total, 1e-30))).astype(BF16)

    def o_copy(yy, d):
        return (
            copy(stat.at[yy], rstat.at[y], st_s.at[d - 1], st_r.at[d - 1], place(x, yy, z, core)),
            copy(obuf.at[yy], robuf.at[y], o_s.at[d - 1], o_r.at[d - 1], place(x, yy, z, core)),
        )

    def o_in(d):
        src = (y + 4 - d) % 4
        return (
            copy(stat.at[src], rstat.at[src], st_s.at[d - 1], st_r.at[d - 1], ydev(4 - d)),
            copy(obuf.at[src], robuf.at[src], o_s.at[d - 1], o_r.at[d - 1], ydev(4 - d)),
        )

    def give(yy):
        @pl.when(yy == y)
        def _():
            robuf[yy] = finished(yy)
            rstat[yy] = stat[yy]

        for d in range(1, 4):

            @pl.when(y + d == yy)
            def _(d=d):
                obuf[yy] = finished(yy)
                for one in o_copy(yy, d):
                    one.start()

    def arrive(t):
        @pl.when(t < 5)
        def _():
            spread_pair(t + 4)

        for n in blocks(t):
            gathered(n)
        za, zb = blocks(t)
        vt[t - 1, pl.ds(0, HS), :] = jnp.concatenate([kv[1, za], kv[1, zb]], axis=0).T
        vt[t - 1, pl.ds(HS, VT - HS), :] = jnp.ones((VT - HS, 2 * HALF), BF16)

    def own_step(t, carry):
        arrive(t)
        attend(t, y, y + 1)
        weight_point(t + 2)
        return carry

    def full_step(t, carry):
        arrive(t)
        attend(t, y, 4)
        weight_point(t + 2)
        return carry

    lax.fori_loop(1, EARLY + 1, own_step, 0)
    for d in range(1, 4):

        @pl.when(y + d <= 3)
        def _(d=d):
            q_in(d).wait_recv()
            turn(y + d)

    lax.fori_loop(EARLY + 1, 9, full_step, 0)

    for yy in (3, 2, 1):

        @pl.when(y < yy)
        def _(yy=yy):
            def one(t, carry):
                attend(t, yy, yy + 1)
                return carry

            lax.fori_loop(1, EARLY + 1, one, 0)

        give(yy)
    give(0)
    for d in range(1, 4):

        @pl.when(y + d <= 3)
        def _(d=d):
            rstat[y + d] = jnp.where(lax.broadcasted_iota(jnp.int32, (8, NQ), 0) < 1, NEG, 0.0).astype(F32)
            robuf[y + d] = jnp.zeros((HS, NQ), BF16)

        @pl.when(y - d >= 0)
        def _(d=d):
            for one in o_in(d):
                one.wait_recv()

    tops = [rstat[yy, pl.ds(0, 1), :] for yy in range(4)]
    best = jnp.maximum(jnp.maximum(tops[0], tops[1]), jnp.maximum(tops[2], tops[3]))
    shares = [rstat[yy, pl.ds(1, 1), :] * jnp.exp2(tops[yy] - best) for yy in range(4)]
    inv = 1.0 / (shares[0] + shares[1] + shares[2] + shares[3])
    mixed = jnp.zeros((HS, NQ), F32)
    for yy in range(4):
        mixed = mixed + robuf[yy].astype(F32) * (shares[yy] * inv)
    send_o[...] = mixed.T.astype(BF16)

    def a_copy(n):
        return copy(
            send_o.at[zrows(n)], att.at[z % 4, zrows(x)], a_s.at[n], a_r.at[x * 4 + z % 4], place(quad, y, n, core)
        )

    def a_in(n):
        sx = n // 4
        return copy(
            send_o.at[zrows(n)], att.at[n % 4, zrows(sx)], a_s.at[n], a_r.at[n], place(sx, y, 4 * fours + n % 4, core)
        )

    def a_send(t, carry):
        a_copy((z + t) % NZ).start()
        a_copy((z + NZ - t) % NZ).start()
        return carry

    lax.fori_loop(1, 8, a_send, 0)
    a_copy((z + 8) % NZ).start()

    @pl.when(quad != x)
    def _():
        a_copy(z).start()

    @pl.when(quad == x)
    def _():
        att[z % 4, zrows(x), :] = send_o[zrows(z), :]

    for slot in range(3):
        ex_copy(slot).wait_send()

    def z_end(d, carry):
        zq_copy(d).wait_send()
        zk_copy(d).wait_send()
        return carry

    lax.fori_loop(1, NZ, z_end, 0)

    def n_end(n, carry):
        for d in range(1, 4):
            xk_copy(n, d).wait_send()

        return carry

    lax.fori_loop(0, NZ, n_end, 0)

    def w_end(i, carry):
        for direction in range(2):
            wz_forward(direction, i).wait_send()
            for d in range(1, 4):
                wy_copy(direction, i, d).wait_send()
        return carry

    lax.fori_loop(0, NP, w_end, 0)
    for d in range(1, 4):

        @pl.when(y - d >= 0)
        def _(d=d):
            q_copy(d).wait_send()

        @pl.when(y + d <= 3)
        def _(d=d):
            for one in o_copy(y + d, d):
                one.wait_send()

    own_weight.wait()

    def wy_wait(n, carry):
        direction, i = n // NP, n % NP
        rows = pl.ds(pl.multiple_of(i * PIECE, PIECE), PIECE)
        for d in range(1, 4):
            c = 2 * ((y + 4 - d) % 4) + direction
            copy(
                wf.at[c, rows], wf.at[c, rows], wy_s.at[direction, i, d - 1], wy_r.at[direction, i, d - 1], ydev(d)
            ).wait_recv()
        return carry

    lax.fori_loop(0, 2 * NP, wy_wait, 0)

    def a_wait(n, carry):
        @pl.when((n // 4 != x) | (4 * fours + n % 4 != z))
        def _():
            a_in(n).wait_recv()

        return carry

    lax.fori_loop(0, NZ, a_wait, 0)

    def c_copy(n):
        return copy(send_c.at[n], recv_c.at[n], c_s.at[n], c_r.at[n], twin)

    def core_rows(n, c):
        return jnp.concatenate(
            [fs[n, pl.ds(pl.multiple_of(xx * 48 + c * ROWS, 8), ROWS), :] for xx in range(4)], axis=0
        )

    def project(n):
        cols = pl.ds(pl.multiple_of(n * CHUNK, 128), CHUNK)
        near = jnp.concatenate([att[2 * zhi], att[2 * zhi + 1]], axis=1)
        far = jnp.concatenate([att[2 - 2 * zhi], att[3 - 2 * zhi]], axis=1)
        fs[n] = jnp.dot(near, w_ref[:, cols], preferred_element_type=F32) + jnp.dot(
            far, wf[n], preferred_element_type=F32
        )
        send_c[n] = core_rows(n, 1 - core).astype(BF16)
        c_copy(n).start()

    def x_copy(g, d):
        to = (x + d) % 4
        return copy(
            send_x.at[g, to], recv_x.at[g, x], x_s.at[g, d - 1], x_r.at[g, d - 1], xdev(d)
        )

    def x_in(g, d):
        src = (x + 4 - d) % 4
        return copy(
            send_x.at[g, src], recv_x.at[g, src], x_s.at[g, d - 1], x_r.at[g, d - 1], xdev(d)
        )

    def pair_sum(g):
        parts = []
        for n in range(2):
            c_copy(2 * g + n).wait_recv()
            parts.append(core_rows(2 * g + n, core) + recv_c[2 * g + n].astype(F32))
        for xx in range(4):
            send_x[g, xx] = jnp.concatenate([part[xx * ROWS : (xx + 1) * ROWS] for part in parts], axis=0).astype(BF16)
        for d in (2, 1, 3):
            x_copy(g, d).start()

    def output_step(g, carry):
        @pl.when(g < 4)
        def _():
            project(2 * g)
            project(2 * g + 1)

        @pl.when(g > 0)
        def _():
            pair_sum(g - 1)

        return carry

    lax.fori_loop(0, 5, output_step, 0)

    def collect(g, carry):
        total = send_x[g, x].astype(F32)
        for d in range(1, 4):
            x_in(g, d).wait_recv()
            total = total + recv_x[g, (x + 4 - d) % 4].astype(F32)
        for n in range(2):
            out_ref[:, pl.ds(pl.multiple_of((2 * g + n) * CHUNK, 128), CHUNK)] = total[n * ROWS : (n + 1) * ROWS]
        return carry

    lax.fori_loop(0, 4, collect, 0)

    def c_end(n, carry):
        c_copy(n).wait_send()
        return carry

    lax.fori_loop(0, 8, c_end, 0)

    def a_end(n, carry):
        @pl.when((n != z) | (quad != x))
        def _():
            a_copy(n).wait_send()

        return carry

    lax.fori_loop(0, NZ, a_end, 0)

    def x_end(g, carry):
        for d in range(1, 4):
            x_copy(g, d).wait_send()
        return carry

    lax.fori_loop(0, 4, x_end, 0)


def last_kernel(proj_ref, gate_ref, lat_ref, step_ref, len_ref, vel_ref, adv_ref):
    span = lax.axis_index("span")
    head = lax.axis_index("head")
    level = step_ref[span]
    length = len_ref[span]

    def sigma_of(step):
        fraction = 1.0 - step / STEPS
        return 8.0 * fraction / (1.0 + 7.0 * fraction)

    now = jnp.full((ROWS, 128), level, jnp.int32).astype(F32)
    dt = sigma_of(now + 1.0) - sigma_of(now)
    spot = head * ROWS + lax.broadcasted_iota(jnp.int32, (ROWS, 128), 0)
    live = jnp.where(spot < length, 1.0, 0.0).astype(F32)
    wide = 512
    dt_w = jnp.concatenate([dt] * (wide // 128), axis=1)
    live_w = jnp.concatenate([live] * (wide // 128), axis=1)
    for n in range(D // wide):
        cols = pl.ds(n * wide, wide)
        gate = gate_ref[pl.ds(level, 1), cols]
        vel = (gate * proj_ref[:, cols] * live_w).astype(BF16)
        vel_ref[:, cols] = vel
        adv_ref[:, cols] = lat_ref[:, cols] + dt_w * vel.astype(F32)


def body(query, keys, values, out_weight, time_gates, noise_step, span_length, window_start, latent):
    vmem = pl.BlockSpec(memory_space=pltpu.VMEM)
    smem = pl.BlockSpec(memory_space=pltpu.SMEM)
    dma = pltpu.SemaphoreType.DMA
    projected = pl.pallas_call(
        main_kernel,
        out_shape=jax.ShapeDtypeStruct((ROWS, D), F32),
        in_specs=[vmem, vmem, vmem, pl.BlockSpec(memory_space=pl.ANY), smem, smem],
        out_specs=vmem,
        scratch_shapes=[
            pltpu.VMEM((256, D), BF16),
            dma,
            pltpu.VMEM((NZ * ROWS, 128), F32),
            pltpu.VMEM((3, NZ * ROWS, 128), BF16),
            pltpu.VMEM((3, NZ * ROWS, 128), BF16),
            pltpu.VMEM((3, NQ, 128), F32),
            pltpu.VMEM((NQ, 128), BF16),
            pltpu.VMEM((2, NQ, 128), BF16),
            pltpu.VMEM((2, NZ, HALF, 128), BF16),
            pltpu.VMEM((8, VT, 2 * HALF), BF16),
            pltpu.VMEM((4, NQ, 128), BF16),
            pltpu.VMEM((4, HS, NQ), BF16),
            pltpu.VMEM((4, ACC, NQ), F32),
            pltpu.VMEM((4, 8, NQ), F32),
            pltpu.VMEM((HALF, 128), jnp.int32),
            pltpu.VMEM((5, 8, NQ), jnp.int32),
            pltpu.VMEM((8, 256, CHUNK), BF16),
            pltpu.VMEM((4, HS, NQ), BF16),
            pltpu.VMEM((4, 8, NQ), F32),
            pltpu.VMEM((4, HS, NQ), BF16),
            pltpu.VMEM((NQ, 128), BF16),
            pltpu.VMEM((4, HALF, 128), BF16),
            pltpu.VMEM((8, HALF, CHUNK), F32),
            pltpu.VMEM((8, 96, CHUNK), BF16),
            pltpu.VMEM((8, 96, CHUNK), BF16),
            pltpu.VMEM((4, 4, 48, CHUNK), BF16),
            pltpu.VMEM((4, 4, 48, CHUNK), BF16),
            dma((3,)), dma((3,)),
            dma((15,)), dma((15,)),
            dma((15,)), dma((15,)),
            dma((NZ, 3)), dma((NZ, 3)),
            dma((3,)), dma((3,)),
            dma((2, NP)), dma((2, NP)),
            dma((2, NP, 3)), dma((2, NP, 3)),
            dma((3,)), dma((3,)),
            dma((3,)), dma((3,)),
            dma((NZ,)), dma((NZ,)),
            dma((8,)), dma((8,)),
            dma((4, 3)), dma((4, 3)),
        ],
        compiler_params=pltpu.CompilerParams(
            collective_id=0, has_side_effects=True, vmem_limit_bytes=40 * 1024 * 1024
        ),
        name="attention_tick",
    )(query, keys, values, out_weight, span_length, window_start)
    return pl.pallas_call(
        last_kernel,
        out_shape=(jax.ShapeDtypeStruct((ROWS, D), BF16), jax.ShapeDtypeStruct((ROWS, D), F32)),
        in_specs=[vmem, vmem, vmem, smem, smem],
        out_specs=(vmem, vmem),
        compiler_params=pltpu.CompilerParams(vmem_limit_bytes=32 * 1024 * 1024),
        name="euler_update",
    )(projected, time_gates, latent, noise_step, span_length)


def solution(mesh):
    rows = P(("span", "head"), None)
    return jax.shard_map(
        body,
        mesh=mesh,
        in_specs=(rows, rows, rows, P("head", None), P(), P(), P(), P(), rows),
        out_specs=(rows, rows),
        check_vma=False,
    )
```
